256 devices in a mesh: grp: 8 (over z), mp: 32 (over x, y, core).
Axes of the slice: x: 4, y: 4, z: 8, core: 2. Of those that a mesh axis runs over, the one named last changes fastest.
Arguments:
- activations: bfloat16 [16, 96, 8192], P('grp', None, 'mp'), may hold values from -6 to 6
- out_grads: bfloat16 [16, 96, 14336], P('grp', None, 'mp'), may hold values from -6 to 6
- valid_counts: int32 [16], P('grp'), may hold values from 24 to 96, as said below
- basis_in: bfloat16 [8192, 8192], P(None, 'mp'), may hold values from -0.0625 to 0.0625
- basis_out: bfloat16 [14336, 14336], P('grp', 'mp'), may hold values from -0.046875 to 0.046875
- eigvals: bfloat16 [14336, 8192], P('mp'), may hold values from 0.3 to 900
- query_out: bfloat16 [8, 16, 14336], P('grp', None, 'mp'), may hold values from -0.01171875 to 0.01171875
- query_in: bfloat16 [8, 16, 8192], P('grp', None, 'mp'), may hold values from -0.0625 to 0.0625
Outputs:
- scores: float32 [16, 8], P('grp')
The draws below stay inside these ranges and needn't reach their ends.
Inputs may be any that keep to these rules, and one draw needn't show every extreme that they name: `valid_counts`: each count is at least a quarter of 96; in every draw some sequence has all 96 slots valid.
All inputs are finite; a program needn't handle non-finite values.
Results may differ from the reference program's by a relative error of at most 0.005.
Values may be sent and summed in bfloat16 or wider, within the bound.
A program may use at most 128 MiB of HBM per device.

```python
import jax
import jax.numpy as jnp
from jax import lax

D = 8192
FF = 14336
LEN = 96
Q = 8
RQ = 16
SEQS = 16


def draw_valid_counts(key, part):
    key = jax.random.fold_in(key, 5)
    values = jax.random.randint(key, (SEQS,), LEN // 4, LEN + 1)
    full_index = jax.random.randint(jax.random.fold_in(key, 1), (), 0, SEQS)
    slots = jnp.arange(SEQS, dtype=jnp.int32)
    return jnp.where(slots == full_index, LEN, values).astype(jnp.int32)


def draw_eigvals(key, part):
    key = jax.random.fold_in(key, 9)
    key_row, key_col, key_entry = jax.random.split(key, 3)
    row_power = jax.random.uniform(key_row, (FF, 1), jnp.float32)
    col_power = jax.random.uniform(key_col, (1, D), jnp.float32)
    ramp = jnp.power(3.0, jnp.arange(FF, dtype=jnp.float32) / FF)[:, None]
    entries = jnp.exp(jnp.clip(0.5 * jax.random.normal(key_entry, (FF, D), jnp.float32), -0.9, 0.9))
    values = ramp * jnp.power(10.0, row_power) * jnp.power(10.0, col_power) * entries
    return values.astype(jnp.bfloat16)


def levels(rng, shape, cuts, smallest, high):
    level = 1.0
    for position, shards_of in cuts:
        draws = jax.random.uniform(jax.random.fold_in(jax.random.fold_in(rng, 6), position), (shards_of,), jnp.float32, smallest / len(cuts), high / len(cuts))
        level = level * jnp.repeat(jnp.exp(draws), shape[position] // shards_of).reshape((-1,) + (1,) * (len(shape) - 1 - position))
    return level


def normal_values(key, dims, width, most, pieces=(), held_as=jnp.bfloat16):
    loudness = levels(key, dims, pieces, -0.22, 0.18) if pieces else 1.0
    array = jax.random.normal(key, dims, jnp.float32) * width * loudness
    return jnp.minimum(jnp.maximum(array, -most), most).astype(held_as)


def setup_inputs(seed: int = 0) -> dict:
    key_of = jax.random.split(jax.random.key(seed), 9)
    activations = normal_values(key_of[0], (SEQS, LEN, D), 1.0, 6.0, ((0, 8), (2, 32)))
    out_grads = normal_values(key_of[1], (SEQS, LEN, FF), 1.0, 6.0, ((0, 8), (2, 32)))
    valid_counts = draw_valid_counts(jax.random.fold_in(key_of[8], 71), 0)
    basis_in = normal_values(key_of[3], (D, D), D ** -0.5, 0.0625, ((1, 32),))
    basis_out = normal_values(key_of[4], (FF, FF), FF ** -0.5, 0.046875, ((0, 8), (1, 32)))
    eigvals = draw_eigvals(jax.random.fold_in(key_of[8], 71), 0)
    query_out = normal_values(key_of[6], (Q, RQ, FF), (FF * RQ) ** -0.5, 0.01171875, ((0, 8), (2, 32)))
    query_in = normal_values(key_of[7], (Q, RQ, D), D ** -0.5, 0.0625, ((0, 8), (2, 32)))
    return dict(activations=activations, out_grads=out_grads, valid_counts=valid_counts, basis_in=basis_in, basis_out=basis_out, eigvals=eigvals, query_out=query_out, query_in=query_in)


def reference(activations, out_grads, valid_counts, basis_in, basis_out, eigvals, query_out, query_in):
    act_rot = jnp.dot(activations.reshape(SEQS * LEN, D), basis_in, preferred_element_type=jnp.float32).astype(jnp.bfloat16).reshape(SEQS, LEN, D)
    positions = jnp.arange(LEN, dtype=jnp.int32)
    keep_mask = (positions[None, :] < valid_counts[:, None]).astype(act_rot.dtype)
    act_kept = act_rot * keep_mask[:, :, None]
    grad_rot = jnp.dot(out_grads.reshape(SEQS * LEN, FF), basis_out, preferred_element_type=jnp.float32).astype(jnp.bfloat16).reshape(SEQS, LEN, FF)
    qin_rot = jnp.dot(query_in.reshape(Q * RQ, D), basis_in, preferred_element_type=jnp.float32).astype(jnp.bfloat16)
    qout_rot = jnp.dot(query_out.reshape(Q * RQ, FF), basis_out, preferred_element_type=jnp.float32).astype(jnp.bfloat16)
    spectrum = eigvals.astype(jnp.float32)
    damping = 0.1 * jnp.sum(spectrum) / (FF * D)
    denominator = spectrum + damping
    qout_wide = qout_rot.astype(jnp.float32)

    def per_sequence(inputs):
        grad_seq, act_seq = inputs
        outer_sum = jnp.dot(grad_seq.T, act_seq, preferred_element_type=jnp.float32)
        weighted = (outer_sum / denominator).astype(jnp.bfloat16)
        mixed_rows = jnp.dot(weighted, qin_rot.T, preferred_element_type=jnp.float32)
        partial_value = jnp.sum(qout_wide.T * mixed_rows, axis=0)
        return jnp.sum(partial_value.reshape(Q, RQ), axis=1)

    return lax.map(per_sequence, (grad_rot, act_kept))
```

```python
import functools

import jax
import jax.numpy as jnp
from jax import lax
from jax.experimental import pallas as pl
from jax.experimental.pallas import tpu as pltpu
from jax.sharding import PartitionSpec as P

MESH = pl.DeviceIdType.MESH
F32 = jnp.float32
BF16 = jnp.bfloat16

SIDE = 4
PLANES = 8
DEVICES = 32
TOKENS = 192
RANK = 16
ROWS = TOKENS + RANK
LEN = 96
HID = 448
FEAT = 256
QROWS = PLANES * RANK
WIDE = TOKENS + QROWS
FF = HID * DEVICES
D = FEAT * DEVICES


def mod(value, n):
    return lax.rem(value + 2 * n, n)


class Gather:
    def __init__(self, place, buf, send_sems, recv_sems):
        self.z, self.m, self.x, self.y, self.core = place
        self.buf, self.send_sems, self.recv_sems = buf, send_sems, recv_sems
        self.p1 = self.x * (1 - self.core) + self.y * self.core
        self.p2 = self.y * (1 - self.core) + self.x * self.core
        self.sibling = self.m + 1 - 2 * self.core
        self.sent = []

    def slot(self, d1, d2):
        a, b = mod(self.p1 + d1, SIDE), mod(self.p2 + d2, SIDE)
        x = a * (1 - self.core) + b * self.core
        y = b * (1 - self.core) + a * self.core
        return (x * SIDE + y) * 2 + self.core

    def copy(self, slot, to, index):
        return pltpu.make_async_remote_copy(
            src_ref=self.buf.at[slot],
            dst_ref=self.buf.at[slot],
            send_sem=self.send_sems.at[index],
            recv_sem=self.recv_sems.at[slot],
            device_id=(self.z, to),
            device_id_type=MESH,
        )

    def send(self, slot, to):
        copy = self.copy(slot, to, len(self.sent))
        copy.start()
        self.sent.append(copy)

    def arrive(self, slot):
        self.copy(slot, self.sibling, 0).wait_recv()

    def event(self, offset, first=(), second=()):
        slot = self.slot(*offset)
        if offset != (0, 0):
            self.arrive(slot)
        for step in first:
            self.send(slot, self.slot(step, 0))
        for step in second:
            self.send(slot, self.slot(0, step))
        self.send(slot, self.sibling)

    def events(self):
        both = (1, -1)
        plan = [
            ((0, 0), both, both),
            ((-1, 0), (1,), both),
            ((1, 0), (), both),
            ((0, -1), (), (1,)),
            ((0, 1), (), ()),
            ((2, 0), (), both),
            ((-1, -1), (), ()),
            ((-1, 1), (), (-1,)),
            ((1, -1), (), ()),
            ((1, 1), (), (-1,)),
            ((2, -1), (), (1,)),
            ((2, 1), (), ()),
            ((0, 2), (), ()),
            ((-1, 2), (), ()),
            ((1, 2), (), ()),
            ((2, 2), (), ()),
        ]
        return [functools.partial(self.event, *entry) for entry in plan]

    def rest(self):
        def body(chip, carry):
            self.arrive(chip * 2 + 1 - self.core)
            return carry

        lax.fori_loop(0, SIDE * SIDE, body, 0)

    def finish(self):
        for copy in self.sent:
            copy.wait_send()


def plane_sum(place, tiles, landed, send_sems, recv_sems):
    z, m, x, y, core = place
    sent = []

    def exchange(stage, base, peers):
        for index, peer in enumerate(peers):
            copy = pltpu.make_async_remote_copy(
                src_ref=tiles.at[stage],
                dst_ref=landed.at[base + index],
                send_sem=send_sems.at[base + index],
                recv_sem=recv_sems.at[base + index],
                device_id=(z, peer),
                device_id_type=MESH,
            )
            copy.start()
            sent.append(copy)
        total = tiles[stage]
        for index in range(len(peers)):
            sent[base + index].wait_recv()
            total = total + landed[base + index]
        return total

    total = exchange(0, 0, [m + 1 - 2 * core])
    tiles[1] = total
    total = exchange(1, 1, [(mod(x + o, SIDE) * SIDE + y) * 2 + core for o in (1, 2, 3)])
    tiles[2] = total
    total = exchange(2, 4, [(x * SIDE + mod(y + o, SIDE)) * 2 + core for o in (1, 2, 3)])
    return total, sent


def kernel(
    acts,
    grads,
    counts,
    basis_in,
    basis_out,
    eigvals,
    query_out,
    query_in,
    out,
    bin_v,
    bout_v,
    eig_v,
    acts_all,
    stage,
    grads_all,
    wide_all,
    acc_in,
    send_a,
    send_b,
    got_a,
    got_b,
    qout_all,
    pad,
    left,
    qout_t,
    mixed,
    tiles1,
    landed1,
    tiles2,
    landed2,
    local_sems,
    acts_send,
    acts_recv,
    grads_send,
    grads_recv,
    wide_send,
    wide_recv,
    perm_sems,
    qin_send,
    qin_recv,
    qout_send,
    qout_recv,
    a_send,
    a_recv,
    b_send,
    b_recv,
    sum1_send,
    sum1_recv,
    sum2_send,
    sum2_recv,
):
    z = lax.axis_index("grp")
    m = lax.axis_index("mp")
    core = lax.rem(m, 2)
    chip = lax.div(m, 2)
    x, y = lax.div(chip, SIDE), lax.rem(chip, SIDE)
    place = (z, m, x, y, core)

    loads = []

    def load(src, dst):
        copy = pltpu.make_async_copy(src, dst, local_sems.at[len(loads)])
        copy.start()
        loads.append(copy)

    load(acts.at[0], acts_all.at[m, pl.ds(0, LEN)])
    load(acts.at[1], acts_all.at[m, pl.ds(LEN, LEN)])
    load(query_in.at[0], acts_all.at[m, pl.ds(TOKENS, RANK)])
    load(grads.at[0], stage.at[pl.ds(0, LEN)])
    load(grads.at[1], stage.at[pl.ds(LEN, LEN)])
    load(query_out.at[0], stage.at[pl.ds(TOKENS, RANK)])
    load(eigvals, eig_v)
    load(basis_in, bin_v)
    load(basis_out, bout_v)

    plane = lax.div(m, 4)
    y_low, y_high = lax.rem(y, 2), lax.div(y, 2)

    def device_of(target, j_high, j_low, source):
        ring = mod(target - source - 4 * j_low, PLANES)
        high = lax.rem(ring, 2)
        low = lax.rem(j_high + lax.rem(target, 2) + high, 2)
        return (lax.div(ring, 2) * SIDE + 2 * high + low) * 2 + j_low

    to = device_of(plane, y_low, core, z)
    from_plane = mod(z - (2 * x + y_high) - 4 * core, PLANES)
    from_device = 4 * z + 2 * lax.rem(y_low + y_high + lax.rem(z, 2), 2) + core
    stays = jnp.logical_and(plane == z, to == m)

    barrier = pltpu.get_barrier_semaphore()
    flat = [(mod(x + o, SIDE) * SIDE + y) * 2 + core for o in (1, 2, 3)]
    flat += [(x * SIDE + mod(y + o, SIDE)) * 2 + core for o in (1, 2, 3)]
    flat.append(m + 1 - 2 * core)
    for peer in flat:
        pl.semaphore_signal(barrier, inc=1, device_id=(z, peer), device_id_type=MESH)
    for o in range(1, PLANES):
        pl.semaphore_signal(
            barrier, inc=1, device_id=(mod(z + o, PLANES), m), device_id_type=MESH
        )

    @pl.when(jnp.logical_not(stays))
    def _():
        pl.semaphore_signal(
            barrier, inc=1, device_id=(from_plane, from_device), device_id_type=MESH
        )

    moves = jnp.where(stays, 0, 1)
    pl.semaphore_wait(barrier, len(flat) + PLANES - 1 + moves)

    permute = pltpu.make_async_remote_copy(
        src_ref=stage,
        dst_ref=grads_all.at[to],
        send_sem=perm_sems.at[0],
        recv_sem=perm_sems.at[1],
        device_id=(plane, to),
        device_id_type=MESH,
    )
    keep = pltpu.make_async_copy(stage, grads_all.at[m], perm_sems.at[2])

    for copy in loads[:3]:
        copy.wait()
    gather_acts = Gather(place, acts_all, acts_send, acts_recv)
    acts_events = gather_acts.events()
    acts_events[0]()
    for copy in loads[3:6]:
        copy.wait()

    @pl.when(stays)
    def _():
        keep.start()

    @pl.when(jnp.logical_not(stays))
    def _():
        permute.start()

    for event in acts_events[1:6]:
        event()

    loads[6].wait()

    def add_eig(slot, total):
        columns = pl.ds(pl.multiple_of(slot * FEAT, FEAT), FEAT)
        block = eig_v[:, columns].astype(F32).reshape(HID // 8, 8, FEAT)
        return total + jnp.sum(block, axis=0)

    eig_sum = lax.fori_loop(0, DEVICES, add_eig, jnp.zeros((8, FEAT), F32))
    tiles1[0] = eig_sum[:, :128] + eig_sum[:, 128:]

    for event in acts_events[6:]:
        event()

    @pl.when(stays)
    def _():
        keep.wait()

    @pl.when(jnp.logical_not(stays))
    def _():
        permute.wait()

    gather_grads = Gather(place, grads_all, grads_send, grads_recv)
    grads_events = gather_grads.events()
    grads_events[0]()

    gather_acts.rest()
    loads[7].wait()
    acc_in[...] = jnp.zeros_like(acc_in)

    def rotate_in(slot, carry):
        rows = pl.ds(pl.multiple_of(slot * FEAT, FEAT), FEAT)
        acc_in[...] += jnp.dot(acts_all[slot], bin_v[rows, :], preferred_element_type=F32)
        return carry

    lax.fori_loop(0, DEVICES, rotate_in, 0)
    position = lax.broadcasted_iota(jnp.int32, (LEN, FEAT), 0)
    for s in range(2):
        rows = pl.ds(s * LEN, LEN)
        kept = jnp.where(position < counts[s], acc_in[rows, :], 0.0)
        wide_all[m, rows, :] = kept.astype(BF16)
    my_query = pl.ds(pl.multiple_of(TOKENS + z * RANK, RANK), RANK)
    wide_all[m, my_query, :] = acc_in[pl.ds(TOKENS, RANK), :].astype(BF16)
    qin_sent = []
    for o in range(1, PLANES):
        copy = pltpu.make_async_remote_copy(
            src_ref=wide_all.at[m, my_query],
            dst_ref=wide_all.at[m, my_query],
            send_sem=qin_send.at[o],
            recv_sem=qin_recv.at[o],
            device_id=(mod(z + o, PLANES), m),
            device_id_type=MESH,
        )
        copy.start()
        qin_sent.append(copy)

    for event in grads_events[1:6]:
        event()
    eig_total, sum1_sent = plane_sum(place, tiles1, landed1, sum1_send, sum1_recv)
    damping = 0.1 * jnp.sum(eig_total) / (FF * D)
    for event in grads_events[6:]:
        event()

    for copy in qin_sent:
        copy.wait_recv()
    gather_wide = Gather(place, wide_all, wide_send, wide_recv)
    wide_events = gather_wide.events()
    wide_events[0]()

    gather_grads.rest()
    loads[8].wait()
    toward = 1 - 2 * core
    ahead = mod(z + toward, PLANES)
    behind = mod(z - toward, PLANES)

    def partial(offset):
        source = mod(z + toward * offset, PLANES)
        total = None
        for j in range(4):
            slot = device_of(z, j // 2, j % 2, source)
            term = jnp.dot(
                grads_all[slot], bout_v[pl.ds(j * HID, HID), :], preferred_element_type=F32
            )
            total = term if total is None else total + term
        return total

    z_sent = []

    def hop(kept, landing, sends, recvs, step, target):
        copy = pltpu.make_async_remote_copy(
            src_ref=kept.at[step],
            dst_ref=landing.at[step],
            send_sem=sends.at[step],
            recv_sem=recvs.at[step],
            device_id=(target, m),
            device_id_type=MESH,
        )
        copy.start()
        z_sent.append(copy)
        return copy

    hop_a = functools.partial(hop, send_a, got_a, a_send, a_recv)
    hop_b = functools.partial(hop, send_b, got_b, b_send, b_recv)
    send_a[0] = partial(4).astype(BF16)
    last_a = hop_a(0, ahead)
    send_b[0] = partial(-3).astype(BF16)
    last_b = hop_b(0, behind)
    wide_queue = wide_events[1:]

    def serve(n):
        for _ in range(n):
            if wide_queue:
                wide_queue.pop(0)()

    for step in (1, 2, 3):
        mine = partial(4 - step)
        serve(2)
        last_a.wait_recv()
        send_a[step] = (mine + got_a[step - 1].astype(F32)).astype(BF16)
        last_a = hop_a(step, ahead)
        if step < 3:
            mine = partial(step - 3)
            serve(2)
            last_b.wait_recv()
            send_b[step] = (mine + got_b[step - 1].astype(F32)).astype(BF16)
            last_b = hop_b(step, behind)
    mine = partial(0)
    serve(len(wide_queue))
    last_b.wait_recv()
    last_a.wait_recv()
    mine = mine + got_b[2].astype(F32) + got_a[3].astype(F32)
    qout_all[pl.ds(pl.multiple_of(z * RANK, RANK), RANK), :] = mine[TOKENS:].astype(BF16)
    qout_sent = []
    for o in range(1, PLANES):
        rows = pl.ds(pl.multiple_of(z * RANK, RANK), RANK)
        copy = pltpu.make_async_remote_copy(
            src_ref=qout_all.at[rows],
            dst_ref=qout_all.at[rows],
            send_sem=qout_send.at[o],
            recv_sem=qout_recv.at[o],
            device_id=(mod(z + o, PLANES), m),
            device_id_type=MESH,
        )
        copy.start()
        qout_sent.append(copy)
    pad[...] = jnp.zeros_like(pad)
    for s in range(2):
        pad[pl.ds(0, LEN), pl.ds(0, HID)] = mine[s * LEN : (s + 1) * LEN]
        left[s] = pad[...].T.astype(BF16)

    gather_wide.rest()
    mixed[...] = jnp.zeros_like(mixed)

    def score(slot, carry):
        columns = pl.ds(pl.multiple_of(slot * FEAT, FEAT), FEAT)
        inverse = 1.0 / (eig_v[:, columns].astype(F32) + damping)
        queries = wide_all[slot, pl.ds(TOKENS, QROWS), :]
        for s in range(2):
            outer = jnp.dot(
                left[s, pl.ds(0, HID), :],
                wide_all[slot, pl.ds(s * LEN, 128), :],
                preferred_element_type=F32,
            )
            weighted = (outer * inverse).astype(BF16)
            mixed[s] += lax.dot_general(
                weighted, queries, (((1,), (1,)), ((), ())), preferred_element_type=F32
            )
        return carry

    lax.fori_loop(0, DEVICES, score, 0)
    for copy in qout_sent:
        copy.wait_recv()
    pad[:, pl.ds(0, HID)] = qout_all[...].astype(F32)
    qout_t[...] = pad[...].T
    tiles2[0] = jnp.zeros((8, 128), F32)
    for s in range(2):
        tiles2[0, pl.ds(s, 1), :] = jnp.sum(
            mixed[s] * qout_t[pl.ds(0, HID), :], axis=0, keepdims=True
        )
    total, sum2_sent = plane_sum(place, tiles2, landed2, sum2_send, sum2_recv)
    out[...] = total

    for gather in (gather_acts, gather_grads, gather_wide):
        gather.finish()
    for copy in qin_sent + qout_sent + z_sent + sum1_sent + sum2_sent:
        copy.wait_send()


def per_device(
    activations, out_grads, valid_counts, basis_in, basis_out, eigvals, query_out, query_in
):
    anywhere = pl.BlockSpec(memory_space=pl.ANY)
    dma = pltpu.SemaphoreType.DMA
    summed = pl.pallas_call(
        kernel,
        out_shape=jax.ShapeDtypeStruct((8, 128), F32),
        in_specs=[anywhere, anywhere, pl.BlockSpec(memory_space=pltpu.SMEM)] + [anywhere] * 5,
        out_specs=pl.BlockSpec(memory_space=pltpu.VMEM),
        scratch_shapes=[
            pltpu.VMEM((D, FEAT), BF16),
            pltpu.VMEM((4 * HID, HID), BF16),
            pltpu.VMEM((HID, D), BF16),
            pltpu.VMEM((DEVICES, ROWS, FEAT), BF16),
            pltpu.VMEM((ROWS, HID), BF16),
            pltpu.VMEM((DEVICES, ROWS, HID), BF16),
            pltpu.VMEM((DEVICES, WIDE, FEAT), BF16),
            pltpu.VMEM((ROWS, FEAT), F32),
            pltpu.VMEM((4, ROWS, HID), BF16),
            pltpu.VMEM((3, ROWS, HID), BF16),
            pltpu.VMEM((4, ROWS, HID), BF16),
            pltpu.VMEM((3, ROWS, HID), BF16),
            pltpu.VMEM((QROWS, HID), BF16),
            pltpu.VMEM((128, 512), F32),
            pltpu.VMEM((2, 512, 128), BF16),
            pltpu.VMEM((512, 128), F32),
            pltpu.VMEM((2, HID, QROWS), F32),
            pltpu.VMEM((3, 8, 128), F32),
            pltpu.VMEM((7, 8, 128), F32),
            pltpu.VMEM((3, 8, 128), F32),
            pltpu.VMEM((7, 8, 128), F32),
            dma((9,)),
            dma((31,)),
            dma((32,)),
            dma((31,)),
            dma((32,)),
            dma((31,)),
            dma((32,)),
            dma((3,)),
            dma((8,)),
            dma((8,)),
            dma((8,)),
            dma((8,)),
            dma((4,)),
            dma((4,)),
            dma((3,)),
            dma((3,)),
            dma((7,)),
            dma((7,)),
            dma((7,)),
            dma((7,)),
        ],
        compiler_params=pltpu.CompilerParams(
            collective_id=0, has_side_effects=True, vmem_limit_bytes=56 * 1024 * 1024
        ),
    )(activations, out_grads, valid_counts, basis_in, basis_out, eigvals, query_out, query_in)
    return jnp.sum(summed[:2].reshape(2, PLANES, RANK), axis=2)


def solution(mesh):
    in_specs = (
        P("grp", None, "mp"),
        P("grp", None, "mp"),
        P("grp"),
        P(None, "mp"),
        P("grp", "mp"),
        P("mp", None),
        P("grp", None, "mp"),
        P("grp", None, "mp"),
    )
    return jax.shard_map(
        per_device, mesh=mesh, in_specs=in_specs, out_specs=P("grp", None), check_vma=False
    )
```

```python
import functools

import jax
import jax.numpy as jnp
from jax import lax
from jax.experimental import pallas as pl
from jax.experimental.pallas import tpu as pltpu
from jax.sharding import PartitionSpec as P

MESH = pl.DeviceIdType.MESH
F32 = jnp.float32
BF16 = jnp.bfloat16

SIDE = 4
PLANES = 8
DEVICES = 32
TOKENS = 192
RANK = 16
ROWS = TOKENS + RANK
LEN = 96
HID = 448
FEAT = 256
QROWS = PLANES * RANK
WIDE = TOKENS + QROWS
FF = HID * DEVICES
D = FEAT * DEVICES


def mod(value, n):
    return lax.rem(value + 2 * n, n)


class Gather:
    def __init__(self, place, buf, send_sems, recv_sems):
        self.z, self.m, self.x, self.y, self.core = place
        self.buf, self.send_sems, self.recv_sems = buf, send_sems, recv_sems
        self.p1 = self.x * (1 - self.core) + self.y * self.core
        self.p2 = self.y * (1 - self.core) + self.x * self.core
        self.sibling = self.m + 1 - 2 * self.core
        self.sent = []

    def slot(self, d1, d2):
        a, b = mod(self.p1 + d1, SIDE), mod(self.p2 + d2, SIDE)
        x = a * (1 - self.core) + b * self.core
        y = b * (1 - self.core) + a * self.core
        return (x * SIDE + y) * 2 + self.core

    def copy(self, slot, to, index):
        return pltpu.make_async_remote_copy(
            src_ref=self.buf.at[slot],
            dst_ref=self.buf.at[slot],
            send_sem=self.send_sems.at[index],
            recv_sem=self.recv_sems.at[slot],
            device_id=(self.z, to),
            device_id_type=MESH,
        )

    def send(self, slot, to):
        copy = self.copy(slot, to, len(self.sent))
        copy.start()
        self.sent.append(copy)

    def arrive(self, slot):
        self.copy(slot, self.sibling, 0).wait_recv()

    def event(self, offset, first=(), second=()):
        slot = self.slot(*offset)
        if offset != (0, 0):
            self.arrive(slot)
        for step in first:
            self.send(slot, self.slot(step, 0))
        for step in second:
            self.send(slot, self.slot(0, step))
        self.send(slot, self.sibling)

    def events(self):
        both = (1, -1)
        plan = [
            ((0, 0), both, both),
            ((-1, 0), (1,), both),
            ((1, 0), (), both),
            ((0, -1), (), (1,)),
            ((0, 1), (), ()),
            ((2, 0), (), both),
            ((-1, -1), (), ()),
            ((-1, 1), (), (-1,)),
            ((1, -1), (), ()),
            ((1, 1), (), (-1,)),
            ((2, -1), (), (1,)),
            ((2, 1), (), ()),
            ((0, 2), (), ()),
            ((-1, 2), (), ()),
            ((1, 2), (), ()),
            ((2, 2), (), ()),
        ]
        return [functools.partial(self.event, *entry) for entry in plan]

    def rest(self):
        def body(chip, carry):
            self.arrive(chip * 2 + 1 - self.core)
            return carry

        lax.fori_loop(0, SIDE * SIDE, body, 0)

    def finish(self):
        for copy in self.sent:
            copy.wait_send()


def plane_sum(place, tiles, landed, send_sems, recv_sems):
    z = place[0]
    row, column = sum_peers(place)
    sent = []

    def exchange(stage, base, peers):
        for index, peer in enumerate(peers):
            copy = pltpu.make_async_remote_copy(
                src_ref=tiles.at[stage],
                dst_ref=landed.at[base + index],
                send_sem=send_sems.at[base + index],
                recv_sem=recv_sems.at[base + index],
                device_id=(z, peer),
                device_id_type=MESH,
            )
            copy.start()
            sent.append(copy)

    def collect(stage, base, peers):
        total = tiles[stage]
        for index in range(len(peers)):
            sent[base + index].wait_recv()
            total = total + landed[base + index]
        return total

    def first():
        exchange(0, 0, row)

    def second():
        tiles[1] = collect(0, 0, row)
        exchange(1, len(row), column)

    def last():
        return collect(1, len(row), column)

    return first, second, last, sent


def sum_peers(place):
    z, m, x, y, core = place
    row = []
    for ox in range(SIDE):
        for oc in range(2):
            if ox or oc:
                row.append((mod(x + ox, SIDE) * SIDE + y) * 2 + lax.rem(core + oc, 2))
    column = [(x * SIDE + mod(y + o, SIDE)) * 2 + core for o in (1, 2, 3)]
    return row, column


HALF = (LEN, LEN + RANK)


def kernel(
    acts,
    grads,
    counts,
    basis_in,
    basis_out,
    eigvals,
    query_out,
    query_in,
    out,
    bin_v,
    bout_t,
    bout_v,
    eig_v,
    inverse,
    acts_all,
    stage0,
    stage1,
    relay0,
    relay1,
    grads0,
    grads1,
    wide_all,
    acc_in,
    send_a0,
    send_b0,
    got_a0,
    got_b0,
    send_a1,
    send_b1,
    got_a1,
    got_b1,
    mine0,
    mine1,
    qout_all,
    pad,
    left,
    qout_t,
    mixed,
    tiles1,
    landed1,
    tiles2,
    landed2,
    local_sems,
    acts_send,
    acts_recv,
    grads_send0,
    grads_recv0,
    grads_send1,
    grads_recv1,
    wide_send,
    wide_recv,
    perm_sems,
    qin_send,
    qin_recv,
    qout_send,
    qout_recv,
    z_send,
    z_recv,
    sum1_send,
    sum1_recv,
    sum2_send,
    sum2_recv,
):
    z = lax.axis_index("grp")
    m = lax.axis_index("mp")
    core = lax.rem(m, 2)
    chip = lax.div(m, 2)
    x, y = lax.div(chip, SIDE), lax.rem(chip, SIDE)
    place = (z, m, x, y, core)
    stage, relay, grads_all = (stage0, stage1), (relay0, relay1), (grads0, grads1)

    loads = []

    def load(src, dst):
        copy = pltpu.make_async_copy(src, dst, local_sems.at[len(loads)])
        copy.start()
        loads.append(copy)

    load(grads.at[0], stage0)
    load(grads.at[1], stage1.at[pl.ds(0, LEN)])
    load(query_out.at[0], stage1.at[pl.ds(LEN, RANK)])
    load(acts.at[0], acts_all.at[m, pl.ds(0, LEN)])
    load(acts.at[1], acts_all.at[m, pl.ds(LEN, LEN)])
    load(query_in.at[0], acts_all.at[m, pl.ds(TOKENS, RANK)])
    load(eigvals, eig_v)
    load(basis_out, bout_t.at[pl.ds(0, HID)])
    load(basis_in, bin_v)

    y_low, y_high = lax.rem(y, 2), lax.div(y, 2)

    def place_of(target, j_high, j_low, source):
        ring = mod(target - source - 4 * j_low, PLANES)
        high = lax.rem(ring, 2)
        low = lax.rem(j_high + lax.rem(target, 2) + high, 2)
        return (lax.div(ring, 2) * SIDE + 2 * high + low) * 2 + j_low

    x_relay = lax.div(mod(2 * x + y_high - z - 4 * core, PLANES), 2)
    relay_to = (x_relay * SIDE + y) * 2 + core
    ring = 2 * x + lax.rem(y_high + z, 2)
    plane = lax.rem(ring + z + 4 * core, PLANES)
    to = place_of(plane, y_low, core, z)
    from_plane = mod(z - (2 * x + y_high) - 4 * core, PLANES)
    from_y = 2 * lax.rem(z, 2) + lax.rem(y_low + y_high + lax.rem(z, 2), 2)
    from_device = (x * SIDE + from_y) * 2 + core
    shifts = x_relay != x
    stays = jnp.logical_and(plane == z, to == m)
    moves = jnp.logical_not(stays)

    barrier = pltpu.get_barrier_semaphore()
    row, column = sum_peers(place)
    for peer in row + column:
        pl.semaphore_signal(barrier, inc=1, device_id=(z, peer), device_id_type=MESH)
    for o in range(1, PLANES):
        pl.semaphore_signal(
            barrier, inc=1, device_id=(mod(z + o, PLANES), m), device_id_type=MESH
        )

    @pl.when(moves)
    def _():
        pl.semaphore_signal(
            barrier, inc=1, device_id=(from_plane, from_device), device_id_type=MESH
        )

    pl.semaphore_wait(
        barrier, len(row) + len(column) + PLANES - 1 + jnp.where(stays, 0, 1)
    )

    shift, shift_here, permute, permute_here = [], [], [], []
    for h in range(2):
        shift.append(
            pltpu.make_async_remote_copy(
                src_ref=stage[h],
                dst_ref=relay[h],
                send_sem=perm_sems.at[h],
                recv_sem=perm_sems.at[2 + h],
                device_id=(z, relay_to),
                device_id_type=MESH,
            )
        )
        shift_here.append(pltpu.make_async_copy(stage[h], relay[h], perm_sems.at[4 + h]))
        permute.append(
            pltpu.make_async_remote_copy(
                src_ref=relay[h],
                dst_ref=grads_all[h].at[to],
                send_sem=perm_sems.at[6 + h],
                recv_sem=perm_sems.at[8 + h],
                device_id=(plane, to),
                device_id_type=MESH,
            )
        )
        permute_here.append(
            pltpu.make_async_copy(relay[h], grads_all[h].at[m], perm_sems.at[10 + h])
        )

    def one_of(predicate, yes, no):
        @pl.when(predicate)
        def _():
            yes()

        @pl.when(jnp.logical_not(predicate))
        def _():
            no()

    for copy in loads[:3]:
        copy.wait()
    for h in range(2):
        one_of(shifts, shift[h].start, shift_here[h].start)
    for copy in loads[3:6]:
        copy.wait()
    gather_acts = Gather(place, acts_all, acts_send, acts_recv)
    gather_grads = [
        Gather(place, grads0, grads_send0, grads_recv0),
        Gather(place, grads1, grads_send1, grads_recv1),
    ]
    gather_wide = Gather(place, wide_all, wide_send, wide_recv)
    acts_queue = gather_acts.events()
    grads_queue = [gather.events() for gather in gather_grads]
    wide_queue = gather_wide.events()

    def serve(queue, n):
        for _ in range(n):
            if queue:
                queue.pop(0)()

    serve(acts_queue, 1)
    for h in range(2):
        one_of(shifts, shift[h].wait, shift_here[h].wait)
        one_of(moves, permute[h].start, permute_here[h].start)

    sum_first, sum_second, sum_last, sum1_sent = plane_sum(
        place, tiles1, landed1, sum1_send, sum1_recv
    )

    def sum_eig():
        loads[6].wait()

        def add_eig(slot, total):
            columns = pl.ds(pl.multiple_of(slot * FEAT, FEAT), FEAT)
            block = eig_v[:, columns].astype(F32).reshape(HID // 8, 8, FEAT)
            return total + jnp.sum(block, axis=0)

        eig_sum = lax.fori_loop(0, DEVICES, add_eig, jnp.zeros((8, FEAT), F32))
        tiles1[0] = eig_sum[:, :128] + eig_sum[:, 128:]
        sum_first()

    def turn_basis():
        loads[7].wait()

        def turn(i, carry):
            rows = pl.ds(pl.multiple_of(i * 128, 128), 128)
            turned = bout_t[:, rows].astype(F32).T
            bout_v[rows, :] = turned[:, :HID].astype(BF16)
            return carry

        lax.fori_loop(0, 4 * HID // 128, turn, 0)

    def invert(start, stop):
        def body(slot, carry):
            columns = pl.ds(pl.multiple_of(slot * FEAT, FEAT), FEAT)
            inverse[slot] = 1.0 / (eig_v[:, columns].astype(F32) + damping)
            return carry

        lax.fori_loop(start, stop, body, 0)

    qin_sent = []
    my_query = pl.ds(pl.multiple_of(TOKENS + z * RANK, RANK), RANK)

    def rotate_in():
        gather_acts.rest()
        loads[8].wait()
        acc_in[...] = jnp.zeros_like(acc_in)

        def body(slot, carry):
            rows = pl.ds(pl.multiple_of(slot * FEAT, FEAT), FEAT)
            acc_in[...] += jnp.dot(acts_all[slot], bin_v[rows, :], preferred_element_type=F32)
            return carry

        lax.fori_loop(0, DEVICES, body, 0)
        position = lax.broadcasted_iota(jnp.int32, (LEN, FEAT), 0)
        for s in range(2):
            rows = pl.ds(s * LEN, LEN)
            kept = jnp.where(position < counts[s], acc_in[rows, :], 0.0)
            wide_all[m, rows, :] = kept.astype(BF16)
        wide_all[m, my_query, :] = acc_in[pl.ds(TOKENS, RANK), :].astype(BF16)
        for o in range(1, PLANES):
            copy = pltpu.make_async_remote_copy(
                src_ref=wide_all.at[m, my_query],
                dst_ref=wide_all.at[m, my_query],
                send_sem=qin_send.at[o],
                recv_sem=qin_recv.at[o],
                device_id=(mod(z + o, PLANES), m),
                device_id_type=MESH,
            )
            copy.start()
            qin_sent.append(copy)

    toward = 1 - 2 * core
    ahead = mod(z + toward, PLANES)
    behind = mod(z - toward, PLANES)
    kept_a, kept_b = (send_a0, send_a1), (send_b0, send_b1)
    landed_a, landed_b = (got_a0, got_a1), (got_b0, got_b1)
    mine = (mine0, mine1)
    z_sent = []
    last = {}

    def pair(h, offsets):
        total = None
        slots = [mod(z + toward * offset, PLANES) for offset in offsets]
        for j in range(4):
            lhs = [grads_all[h][place_of(z, j // 2, j % 2, source)] for source in slots]
            term = jnp.dot(
                jnp.concatenate(lhs, axis=0),
                bout_v[pl.ds(j * HID, HID), :],
                preferred_element_type=F32,
            )
            total = term if total is None else total + term
        return total[: HALF[h]], total[HALF[h] :]

    def hop(h, way, step):
        index = h * 7 + way * 4 + step
        copy = pltpu.make_async_remote_copy(
            src_ref=(kept_a, kept_b)[way][h].at[step],
            dst_ref=(landed_a, landed_b)[way][h].at[step],
            send_sem=z_send.at[index],
            recv_sem=z_recv.at[index],
            device_id=((ahead, behind)[way], m),
            device_id_type=MESH,
        )
        copy.start()
        z_sent.append(copy)
        last[h, way] = copy

    def reduce_step(h, step):
        if step == 0:
            a, b = pair(h, (4, -3))
            kept_a[h][0] = a.astype(BF16)
            hop(h, 0, 0)
            kept_b[h][0] = b.astype(BF16)
            hop(h, 1, 0)
        elif step < 3:
            a, b = pair(h, (4 - step, step - 3))
            last[h, 0].wait_recv()
            kept_a[h][step] = (a + landed_a[h][step - 1].astype(F32)).astype(BF16)
            hop(h, 0, step)
            last[h, 1].wait_recv()
            kept_b[h][step] = (b + landed_b[h][step - 1].astype(F32)).astype(BF16)
            hop(h, 1, step)
        elif step == 3:
            a, b = pair(h, (1, 0))
            last[h, 0].wait_recv()
            kept_a[h][3] = (a + landed_a[h][2].astype(F32)).astype(BF16)
            hop(h, 0, 3)
            last[h, 1].wait_recv()
            mine[h][...] = b + landed_b[h][2].astype(F32)
        else:
            last[h, 0].wait_recv()
            mine[h][...] += landed_a[h][3].astype(F32)
            pad[pl.ds(0, LEN), pl.ds(0, HID)] = mine[h][pl.ds(0, LEN), :]
            left[h] = pad[...].T.astype(BF16)

    pad[...] = jnp.zeros_like(pad)
    serve(acts_queue, 5)
    sum_eig()
    serve(acts_queue, 4)
    for h in range(2):
        one_of(moves, permute[h].wait, permute_here[h].wait)
        serve(grads_queue[h], 1)
    serve(acts_queue, 6)
    serve(grads_queue[0], 5)
    sum_second()
    turn_basis()
    serve(grads_queue[0], 4)
    rotate_in()
    serve(grads_queue[0], 6)
    serve(grads_queue[1], 5)
    damping = 0.1 * jnp.sum(sum_last()) / (FF * D)
    gather_grads[0].rest()
    reduce_step(0, 0)
    serve(grads_queue[1], 4)
    invert(0, 8)
    reduce_step(0, 1)
    serve(grads_queue[1], 3)
    for copy in qin_sent:
        copy.wait_recv()
    serve(wide_queue, 1)
    serve(grads_queue[1], 3)
    reduce_step(0, 2)
    serve(wide_queue, 2)
    gather_grads[1].rest()
    reduce_step(1, 0)
    serve(wide_queue, 3)
    reduce_step(0, 3)
    invert(8, 16)
    reduce_step(1, 1)
    serve(wide_queue, 3)
    reduce_step(0, 4)
    invert(16, 24)
    reduce_step(1, 2)
    serve(wide_queue, 4)
    invert(24, 32)
    reduce_step(1, 3)
    serve(wide_queue, 3)
    reduce_step(1, 4)

    my_rows = pl.ds(pl.multiple_of(z * RANK, RANK), RANK)
    qout_all[my_rows, :] = mine1[pl.ds(LEN, RANK), :].astype(BF16)
    qout_sent = []
    for o in range(1, PLANES):
        copy = pltpu.make_async_remote_copy(
            src_ref=qout_all.at[my_rows],
            dst_ref=qout_all.at[my_rows],
            send_sem=qout_send.at[o],
            recv_sem=qout_recv.at[o],
            device_id=(mod(z + o, PLANES), m),
            device_id_type=MESH,
        )
        copy.start()
        qout_sent.append(copy)

    gather_wide.rest()
    mixed[...] = jnp.zeros_like(mixed)

    def score(slot, carry):
        queries = wide_all[slot, pl.ds(TOKENS, QROWS), :]
        for s in range(2):
            outer = jnp.dot(
                left[s, pl.ds(0, HID), :],
                wide_all[slot, pl.ds(s * LEN, 128), :],
                preferred_element_type=F32,
            )
            weighted = (outer * inverse[slot]).astype(BF16)
            mixed[s] += lax.dot_general(
                weighted, queries, (((1,), (1,)), ((), ())), preferred_element_type=F32
            )
        return carry

    lax.fori_loop(0, DEVICES, score, 0)
    for copy in qout_sent:
        copy.wait_recv()
    pad[:, pl.ds(0, HID)] = qout_all[...].astype(F32)
    qout_t[...] = pad[...].T
    tiles2[0] = jnp.zeros((8, 128), F32)
    for s in range(2):
        tiles2[0, pl.ds(s, 1), :] = jnp.sum(
            mixed[s] * qout_t[pl.ds(0, HID), :], axis=0, keepdims=True
        )
    end_first, end_second, end_last, sum2_sent = plane_sum(
        place, tiles2, landed2, sum2_send, sum2_recv
    )
    end_first()
    end_second()
    out[...] = end_last()[:2]

    for gather in (gather_acts, *gather_grads, gather_wide):
        gather.finish()
    for copy in qin_sent + qout_sent + z_sent + sum1_sent + sum2_sent:
        copy.wait_send()


def per_device(
    activations, out_grads, valid_counts, basis_in, basis_out, eigvals, query_out, query_in
):
    anywhere = pl.BlockSpec(memory_space=pl.ANY)
    dma = pltpu.SemaphoreType.DMA
    halves = [
        pltpu.VMEM((count, rows, HID), BF16)
        for rows in HALF
        for count in (4, 3, 4, 3)
    ]
    gather_sems = [dma((31,)), dma((32,))]
    summed = pl.pallas_call(
        kernel,
        out_shape=jax.ShapeDtypeStruct((2, 128), F32),
        in_specs=[anywhere, anywhere, pl.BlockSpec(memory_space=pltpu.SMEM)] + [anywhere] * 5,
        out_specs=pl.BlockSpec(memory_space=pltpu.VMEM),
        scratch_shapes=[
            pltpu.VMEM((D, FEAT), BF16),
            pltpu.VMEM((512, 4 * HID), BF16),
            pltpu.VMEM((4 * HID, HID), BF16),
            pltpu.VMEM((HID, D), BF16),
            pltpu.VMEM((DEVICES, HID, FEAT), F32),
            pltpu.VMEM((DEVICES, ROWS, FEAT), BF16),
            pltpu.VMEM((HALF[0], HID), BF16),
            pltpu.VMEM((HALF[1], HID), BF16),
            pltpu.VMEM((HALF[0], HID), BF16),
            pltpu.VMEM((HALF[1], HID), BF16),
            pltpu.VMEM((DEVICES, HALF[0], HID), BF16),
            pltpu.VMEM((DEVICES, HALF[1], HID), BF16),
            pltpu.VMEM((DEVICES, WIDE, FEAT), BF16),
            pltpu.VMEM((ROWS, FEAT), F32),
            *halves,
            pltpu.VMEM((HALF[0], HID), F32),
            pltpu.VMEM((HALF[1], HID), F32),
            pltpu.VMEM((QROWS, HID), BF16),
            pltpu.VMEM((128, 512), F32),
            pltpu.VMEM((2, 512, 128), BF16),
            pltpu.VMEM((512, 128), F32),
            pltpu.VMEM((2, HID, QROWS), F32),
            pltpu.VMEM((2, 8, 128), F32),
            pltpu.VMEM((10, 8, 128), F32),
            pltpu.VMEM((2, 8, 128), F32),
            pltpu.VMEM((10, 8, 128), F32),
            dma((9,)),
            *gather_sems * 4,
            dma((12,)),
            dma((8,)),
            dma((8,)),
            dma((8,)),
            dma((8,)),
            dma((14,)),
            dma((14,)),
            dma((10,)),
            dma((10,)),
            dma((10,)),
            dma((10,)),
        ],
        compiler_params=pltpu.CompilerParams(
            collective_id=0, has_side_effects=True, vmem_limit_bytes=60 * 1024 * 1024
        ),
    )(activations, out_grads, valid_counts, basis_in, basis_out.T, eigvals, query_out, query_in)
    return jnp.sum(summed.reshape(2, PLANES, RANK), axis=2)


def solution(mesh):
    in_specs = (
        P("grp", None, "mp"),
        P("grp", None, "mp"),
        P("grp"),
        P(None, "mp"),
        P("grp", "mp"),
        P("mp", None),
        P("grp", None, "mp"),
        P("grp", None, "mp"),
    )
    return jax.shard_map(
        per_device, mesh=mesh, in_specs=in_specs, out_specs=P("grp", None), check_vma=False
    )
```

```python
import functools

import jax
import jax.numpy as jnp
from jax import lax
from jax.experimental import pallas as pl
from jax.experimental.pallas import tpu as pltpu
from jax.sharding import PartitionSpec as P

MESH = pl.DeviceIdType.MESH
F32 = jnp.float32
BF16 = jnp.bfloat16

SIDE = 4
PLANES = 8
DEVICES = 32
TOKENS = 192
RANK = 16
ROWS = TOKENS + RANK
LEN = 96
HID = 448
FEAT = 256
QROWS = PLANES * RANK
WIDE = TOKENS + QROWS
FF = HID * DEVICES
D = FEAT * DEVICES


def mod(value, n):
    return lax.rem(value + 2 * n, n)


BOTH = (1, -1)
RING = (
    ((0, 0), BOTH, BOTH),
    ((-1, 0), (1,), BOTH),
    ((1, 0), (), BOTH),
    ((0, -1), (), (1,)),
    ((0, 1), (), ()),
    ((2, 0), (), BOTH),
    ((-1, -1), (), ()),
    ((-1, 1), (), (-1,)),
    ((1, -1), (), ()),
    ((1, 1), (), (-1,)),
    ((2, -1), (), (1,)),
    ((2, 1), (), ()),
    ((0, 2), (), ()),
    ((-1, 2), (), ()),
    ((1, 2), (), ()),
    ((2, 2), (), ()),
)
EARLY = (((0, 0), (1, -1, 2), BOTH), ((-1, 0), (), BOTH)) + RING[2:]
GROUPS = (0, -1, 1, 2)


def slot_of(x, y, core, d1, d2):
    a = mod(x * (1 - core) + y * core + d1, SIDE)
    b = mod(y * (1 - core) + x * core + d2, SIDE)
    return ((a * (1 - core) + b * core) * SIDE + b * (1 - core) + a * core) * 2 + core


class Gather:
    def __init__(self, place, buf, send_sems, recv_sems):
        self.z, self.m, self.x, self.y, self.core = place
        self.buf, self.send_sems, self.recv_sems = buf, send_sems, recv_sems
        self.sibling = self.m + 1 - 2 * self.core
        self.sent = []

    def slot(self, d1, d2):
        return slot_of(self.x, self.y, self.core, d1, d2)

    def copy(self, slot, to, index):
        return pltpu.make_async_remote_copy(
            src_ref=self.buf.at[slot],
            dst_ref=self.buf.at[slot],
            send_sem=self.send_sems.at[index],
            recv_sem=self.recv_sems.at[slot],
            device_id=(self.z, to),
            device_id_type=MESH,
        )

    def send(self, slot, to):
        copy = self.copy(slot, to, len(self.sent))
        copy.start()
        self.sent.append(copy)

    def arrive(self, slot):
        self.copy(slot, self.sibling, 0).wait_recv()

    def event(self, offset, first=(), second=()):
        slot = self.slot(*offset)
        if offset != (0, 0):
            self.arrive(slot)
        for step in first:
            self.send(slot, self.slot(step, 0))
        for step in second:
            self.send(slot, self.slot(0, step))
        self.send(slot, self.sibling)

    def events(self, plan):
        return [functools.partial(self.event, *entry) for entry in plan]

    def group(self, d1):
        def body(d2, carry):
            self.arrive(slot_of(self.x, self.y, 1 - self.core, d1, d2))
            return carry

        lax.fori_loop(0, SIDE, body, 0)

    def rest(self):
        def body(chip, carry):
            self.arrive(chip * 2 + 1 - self.core)
            return carry

        lax.fori_loop(0, SIDE * SIDE, body, 0)

    def finish(self):
        for copy in self.sent:
            copy.wait_send()


def plane_sum(place, tiles, landed, send_sems, recv_sems):
    z = place[0]
    row, column = sum_peers(place)
    sent = []

    def exchange(stage, base, peers):
        for index, peer in enumerate(peers):
            copy = pltpu.make_async_remote_copy(
                src_ref=tiles.at[stage],
                dst_ref=landed.at[base + index],
                send_sem=send_sems.at[base + index],
                recv_sem=recv_sems.at[base + index],
                device_id=(z, peer),
                device_id_type=MESH,
            )
            copy.start()
            sent.append(copy)

    def collect(stage, base, peers):
        total = tiles[stage]
        for index in range(len(peers)):
            sent[base + index].wait_recv()
            total = total + landed[base + index]
        return total

    def first():
        exchange(0, 0, row)

    def second():
        tiles[1] = collect(0, 0, row)
        exchange(1, len(row), column)

    def last():
        return collect(1, len(row), column)

    return first, second, last, sent


def sum_peers(place):
    z, m, x, y, core = place
    row = []
    for ox in range(SIDE):
        for oc in range(2):
            if ox or oc:
                row.append((mod(x + ox, SIDE) * SIDE + y) * 2 + lax.rem(core + oc, 2))
    column = [(x * SIDE + mod(y + o, SIDE)) * 2 + core for o in (1, 2, 3)]
    return row, column


PLAN_A, PLAN_G, PLAN_W = RING, EARLY, RING
SCHEDULE = (
    "sG", "sH", "A0", "turn", "eig", "rG", "rH", "A1", "A2", "A3", "A4", "eig2", "A5", "A7",
    "tG", "G0", "A6", "A9", "A8", "A12", "damp", "tH", "H0", "A11", "A10", "inv0", "A13", "G1",
    "rot0", "G2", "inv1", "G5", "G3", "G4", "rot1", "inv2", "A14", "H1", "inv3", "H2", "H3",
    "rot2", "H5", "A15", "H4", "G6", "G7", "rot3", "G8", "rotd", "G9", "G10", "G11", "G12",
    "H7", "H6", "H9", "W0", "H8", "H11", "H12", "G13", "H10", "G14", "G15", "H13", "W1", "zG0",
    "pG1", "H14", "W2", "W3", "H15", "W4", "W5", "zH0", "zG1", "pG2", "pH1", "W6", "W7", "W9",
    "W8", "W11", "W12", "zH1", "pH2", "W10", "W13", "zG2", "pG3", "W14", "zH2", "pH3", "W15",
    "zG3", "zH3", "zG4", "sc00", "sc01", "sc02", "zH4", "sc03", "sc10", "sc11", "qt", "sc12",
    "sc13",
)
HALF = (LEN, LEN + RANK)


def kernel(
    acts,
    grads,
    counts,
    basis_in,
    basis_out,
    eigvals,
    query_out,
    query_in,
    out,
    bin_v,
    bout_t,
    bout_v,
    eig_v,
    inverse,
    acts_all,
    stage0,
    stage1,
    relay0,
    relay1,
    grads0,
    grads1,
    wide_all,
    acc_in,
    send_a0,
    send_b0,
    got_a0,
    got_b0,
    send_a1,
    send_b1,
    got_a1,
    got_b1,
    mine0,
    mine1,
    qout_all,
    pad,
    left,
    qout_t,
    mixed,
    weighted,
    tiles1,
    landed1,
    tiles2,
    landed2,
    local_sems,
    acts_send,
    acts_recv,
    grads_send0,
    grads_recv0,
    grads_send1,
    grads_recv1,
    wide_send,
    wide_recv,
    perm_sems,
    qin_send,
    qin_recv,
    qout_send,
    qout_recv,
    z_send,
    z_recv,
    sum1_send,
    sum1_recv,
    sum2_send,
    sum2_recv,
):
    z = lax.axis_index("grp")
    m = lax.axis_index("mp")
    core = lax.rem(m, 2)
    chip = lax.div(m, 2)
    x, y = lax.div(chip, SIDE), lax.rem(chip, SIDE)
    place = (z, m, x, y, core)
    stage, relay, grads_all = (stage0, stage1), (relay0, relay1), (grads0, grads1)

    loads = []

    def load(src, dst):
        copy = pltpu.make_async_copy(src, dst, local_sems.at[len(loads)])
        copy.start()
        loads.append(copy)

    load(grads.at[0], stage0)
    load(grads.at[1], stage1.at[pl.ds(0, LEN)])
    load(query_out.at[0], stage1.at[pl.ds(LEN, RANK)])
    load(acts.at[0], acts_all.at[m, pl.ds(0, LEN)])
    load(acts.at[1], acts_all.at[m, pl.ds(LEN, LEN)])
    load(query_in.at[0], acts_all.at[m, pl.ds(TOKENS, RANK)])
    load(eigvals, eig_v)
    load(basis_out, bout_t.at[pl.ds(0, HID)])
    load(basis_in, bin_v)

    y_low, y_high = lax.rem(y, 2), lax.div(y, 2)

    def place_of(target, j_high, j_low, source):
        ring = mod(target - source - 4 * j_low, PLANES)
        high = lax.rem(ring, 2)
        low = lax.rem(j_high + lax.rem(target, 2) + high, 2)
        return (lax.div(ring, 2) * SIDE + 2 * high + low) * 2 + j_low

    x_relay = lax.div(mod(2 * x + y_high - z - 4 * core, PLANES), 2)
    relay_to = (x_relay * SIDE + y) * 2 + core
    ring = 2 * x + lax.rem(y_high + z, 2)
    plane = lax.rem(ring + z + 4 * core, PLANES)
    to = place_of(plane, y_low, core, z)
    from_plane = mod(z - (2 * x + y_high) - 4 * core, PLANES)
    from_y = 2 * lax.rem(z, 2) + lax.rem(y_low + y_high + lax.rem(z, 2), 2)
    from_device = (x * SIDE + from_y) * 2 + core
    shifts = x_relay != x
    stays = jnp.logical_and(plane == z, to == m)
    moves = jnp.logical_not(stays)

    barrier = pltpu.get_barrier_semaphore()
    row, column = sum_peers(place)
    for peer in row + column:
        pl.semaphore_signal(barrier, inc=1, device_id=(z, peer), device_id_type=MESH)
    for o in range(1, PLANES):
        pl.semaphore_signal(
            barrier, inc=1, device_id=(mod(z + o, PLANES), m), device_id_type=MESH
        )

    @pl.when(moves)
    def _():
        pl.semaphore_signal(
            barrier, inc=1, device_id=(from_plane, from_device), device_id_type=MESH
        )

    pl.semaphore_wait(
        barrier, len(row) + len(column) + PLANES - 1 + jnp.where(stays, 0, 1)
    )

    shift, shift_here, permute, permute_here = [], [], [], []
    for h in range(2):
        shift.append(
            pltpu.make_async_remote_copy(
                src_ref=stage[h],
                dst_ref=relay[h],
                send_sem=perm_sems.at[h],
                recv_sem=perm_sems.at[2 + h],
                device_id=(z, relay_to),
                device_id_type=MESH,
            )
        )
        shift_here.append(pltpu.make_async_copy(stage[h], relay[h], perm_sems.at[4 + h]))
        permute.append(
            pltpu.make_async_remote_copy(
                src_ref=relay[h],
                dst_ref=grads_all[h].at[to],
                send_sem=perm_sems.at[6 + h],
                recv_sem=perm_sems.at[8 + h],
                device_id=(plane, to),
                device_id_type=MESH,
            )
        )
        permute_here.append(
            pltpu.make_async_copy(relay[h], grads_all[h].at[m], perm_sems.at[10 + h])
        )

    def one_of(predicate, yes, no):
        @pl.when(predicate)
        def _():
            yes()

        @pl.when(jnp.logical_not(predicate))
        def _():
            no()

    for copy in loads[:6]:
        copy.wait()
    gather_acts = Gather(place, acts_all, acts_send, acts_recv)
    gather_grads = [
        Gather(place, grads0, grads_send0, grads_recv0),
        Gather(place, grads1, grads_send1, grads_recv1),
    ]
    gather_wide = Gather(place, wide_all, wide_send, wide_recv)
    run = {}
    for letter, gather, plan in (
        ("A", gather_acts, PLAN_A),
        ("G", gather_grads[0], PLAN_G),
        ("H", gather_grads[1], PLAN_G),
        ("W", gather_wide, PLAN_W),
    ):
        for index, event in enumerate(gather.events(plan)):
            run[letter + str(index)] = event

    def relay_block(h):
        one_of(shifts, shift[h].wait, shift_here[h].wait)
        one_of(moves, permute[h].start, permute_here[h].start)

    def take_block(h):
        one_of(moves, permute[h].wait, permute_here[h].wait)

    sum_first, sum_second, sum_last, sum1_sent = plane_sum(
        place, tiles1, landed1, sum1_send, sum1_recv
    )

    def sum_eig():
        loads[6].wait()

        def add_eig(slot, total):
            columns = pl.ds(pl.multiple_of(slot * FEAT, FEAT), FEAT)
            block = eig_v[:, columns].astype(F32).reshape(HID // 8, 8, FEAT)
            return total + jnp.sum(block, axis=0)

        eig_sum = lax.fori_loop(0, DEVICES, add_eig, jnp.zeros((8, FEAT), F32))
        tiles1[0] = eig_sum[:, :128] + eig_sum[:, 128:]
        sum_first()

    def turn_basis():
        loads[7].wait()

        def turn(i, carry):
            rows = pl.ds(pl.multiple_of(i * 128, 128), 128)
            turned = bout_t[:, rows].astype(F32).T
            bout_v[rows, :] = turned[:, :HID].astype(BF16)
            return carry

        lax.fori_loop(0, 4 * HID // 128, turn, 0)

    def invert(start, stop):
        def body(slot, carry):
            columns = pl.ds(pl.multiple_of(slot * FEAT, FEAT), FEAT)
            inverse[slot] = 1.0 / (eig_v[:, columns].astype(F32) + scale[0])
            return carry

        lax.fori_loop(start, stop, body, 0)

    qin_sent = []
    my_query = pl.ds(pl.multiple_of(TOKENS + z * RANK, RANK), RANK)

    def group_slots(group):
        return [
            slot_of(x, y, lax.rem(core + k, 2), GROUPS[group], k // 2) for k in range(2 * SIDE)
        ]

    def rotate_group(group):
        gather_acts.group(GROUPS[group])
        if group == 0:
            loads[8].wait()
            acc_in[...] = jnp.zeros_like(acc_in)

        total = None
        for slot in group_slots(group):
            rows = pl.ds(pl.multiple_of(slot * FEAT, FEAT), FEAT)
            term = jnp.dot(acts_all[slot], bin_v[rows, :], preferred_element_type=F32)
            total = term if total is None else total + term
        acc_in[...] += total

    def rotated():
        position = lax.broadcasted_iota(jnp.int32, (LEN, FEAT), 0)
        for s in range(2):
            rows = pl.ds(s * LEN, LEN)
            kept = jnp.where(position < counts[s], acc_in[rows, :], 0.0)
            wide_all[m, rows, :] = kept.astype(BF16)
        wide_all[m, my_query, :] = acc_in[pl.ds(TOKENS, RANK), :].astype(BF16)
        for o in range(1, PLANES):
            copy = pltpu.make_async_remote_copy(
                src_ref=wide_all.at[m, my_query],
                dst_ref=wide_all.at[m, my_query],
                send_sem=qin_send.at[o],
                recv_sem=qin_recv.at[o],
                device_id=(mod(z + o, PLANES), m),
                device_id_type=MESH,
            )
            copy.start()
            qin_sent.append(copy)

    toward = 1 - 2 * core
    ahead = mod(z + toward, PLANES)
    behind = mod(z - toward, PLANES)
    kept_a, kept_b = (send_a0, send_a1), (send_b0, send_b1)
    landed_a, landed_b = (got_a0, got_a1), (got_b0, got_b1)
    mine = (mine0, mine1)
    z_sent = []
    last = {}

    def pair(h, offsets):
        total = None
        slots = [mod(z + toward * offset, PLANES) for offset in offsets]
        for j in range(4):
            lhs = [grads_all[h][place_of(z, j // 2, j % 2, source)] for source in slots]
            term = jnp.dot(
                jnp.concatenate(lhs, axis=0),
                bout_v[pl.ds(j * HID, HID), :],
                preferred_element_type=F32,
            )
            total = term if total is None else total + term
        return total[: HALF[h]], total[HALF[h] :]

    def hop(h, way, step):
        index = h * 7 + way * 4 + step
        copy = pltpu.make_async_remote_copy(
            src_ref=(kept_a, kept_b)[way][h].at[step],
            dst_ref=(landed_a, landed_b)[way][h].at[step],
            send_sem=z_send.at[index],
            recv_sem=z_recv.at[index],
            device_id=((ahead, behind)[way], m),
            device_id_type=MESH,
        )
        copy.start()
        z_sent.append(copy)
        last[h, way] = copy

    products = {}

    def product(h, step):
        products[h] = pair(h, ((4, -3), (3, -2), (2, -1), (1, 0))[step])

    def reduce_step(h, step):
        if step == 0:
            gather_grads[h].rest()
            product(h, 0)
            a, b = products[h]
            kept_a[h][0] = a.astype(BF16)
            hop(h, 0, 0)
            kept_b[h][0] = b.astype(BF16)
            hop(h, 1, 0)
        elif step < 4:
            a, b = products[h]
            last[h, 0].wait_recv()
            kept_a[h][step] = (a + landed_a[h][step - 1].astype(F32)).astype(BF16)
            hop(h, 0, step)
            last[h, 1].wait_recv()
            b = b + landed_b[h][step - 1].astype(F32)
            if step < 3:
                kept_b[h][step] = b.astype(BF16)
                hop(h, 1, step)
            else:
                mine[h][...] = b
        else:
            last[h, 0].wait_recv()
            mine[h][...] += landed_a[h][3].astype(F32)
            pad[pl.ds(0, LEN), pl.ds(0, HID)] = mine[h][pl.ds(0, LEN), :]
            left[h] = pad[...].T.astype(BF16)
            if h:
                send_qout()

    my_rows = pl.ds(pl.multiple_of(z * RANK, RANK), RANK)
    qout_sent = []

    def send_qout():
        qout_all[my_rows, :] = mine1[pl.ds(LEN, RANK), :].astype(BF16)
        for o in range(1, PLANES):
            copy = pltpu.make_async_remote_copy(
                src_ref=qout_all.at[my_rows],
                dst_ref=qout_all.at[my_rows],
                send_sem=qout_send.at[o],
                recv_sem=qout_recv.at[o],
                device_id=(mod(z + o, PLANES), m),
                device_id_type=MESH,
            )
            copy.start()
            qout_sent.append(copy)

    arrived = set()

    def score(s, group):
        if group not in arrived:
            arrived.add(group)
            gather_wide.group(GROUPS[group])

        slots = group_slots(group)
        for k, slot in enumerate(slots):
            outer = jnp.dot(
                left[s, pl.ds(0, HID), :],
                wide_all[slot, pl.ds(s * LEN, 128), :],
                preferred_element_type=F32,
            )
            weighted[:, pl.ds(k * FEAT, FEAT)] = (outer * inverse[slot]).astype(BF16)
        queries = [wide_all[slot, pl.ds(TOKENS, QROWS), :] for slot in slots]
        mixed[s] += lax.dot_general(
            weighted[...],
            jnp.concatenate(queries, axis=1),
            (((1,), (1,)), ((), ())),
            preferred_element_type=F32,
        )

    def turn_queries():
        for copy in qout_sent:
            copy.wait_recv()
        pad[:, pl.ds(0, HID)] = qout_all[...].astype(F32)
        qout_t[...] = pad[...].T

    def start_wide():
        for copy in qin_sent:
            copy.wait_recv()
        run["W"]()

    scale = []

    def damp():
        scale.append(0.1 * jnp.sum(sum_last()) / (FF * D))

    run["W"], run["W0"] = run["W0"], start_wide
    for h, letter in enumerate("GH"):
        run["s" + letter] = functools.partial(one_of, shifts, shift[h].start, shift_here[h].start)
        run["r" + letter] = functools.partial(relay_block, h)
        run["t" + letter] = functools.partial(take_block, h)
        for step in range(5):
            run["z" + letter + str(step)] = functools.partial(reduce_step, h, step)
            run["p" + letter + str(step)] = functools.partial(product, h, step)
    for group in range(SIDE):
        run["rot" + str(group)] = functools.partial(rotate_group, group)
        run["inv" + str(group)] = functools.partial(invert, 8 * group, 8 * group + 8)
        for s in range(2):
            run["sc" + str(s) + str(group)] = functools.partial(score, s, group)
    run.update(eig=sum_eig, eig2=sum_second, turn=turn_basis, damp=damp, qt=turn_queries, rotd=rotated)

    pad[...] = jnp.zeros_like(pad)
    mixed[...] = jnp.zeros_like(mixed)
    for name in SCHEDULE:
        run[name]()

    tiles2[0] = jnp.zeros((8, 128), F32)
    for s in range(2):
        tiles2[0, pl.ds(s, 1), :] = jnp.sum(
            mixed[s] * qout_t[pl.ds(0, HID), :], axis=0, keepdims=True
        )
    end_first, end_second, end_last, sum2_sent = plane_sum(
        place, tiles2, landed2, sum2_send, sum2_recv
    )
    end_first()
    end_second()
    out[...] = end_last()[:2]

    for gather in (gather_acts, *gather_grads, gather_wide):
        gather.finish()
    for copy in qin_sent + qout_sent + z_sent + sum1_sent + sum2_sent:
        copy.wait_send()


def per_device(
    activations, out_grads, valid_counts, basis_in, basis_out, eigvals, query_out, query_in
):
    anywhere = pl.BlockSpec(memory_space=pl.ANY)
    dma = pltpu.SemaphoreType.DMA
    halves = [
        pltpu.VMEM((count, rows, HID), BF16)
        for rows in HALF
        for count in (4, 3, 4, 3)
    ]
    gather_sems = [dma((31,)), dma((32,))]
    summed = pl.pallas_call(
        kernel,
        out_shape=jax.ShapeDtypeStruct((2, 128), F32),
        in_specs=[anywhere, anywhere, pl.BlockSpec(memory_space=pltpu.SMEM)] + [anywhere] * 5,
        out_specs=pl.BlockSpec(memory_space=pltpu.VMEM),
        scratch_shapes=[
            pltpu.VMEM((D, FEAT), BF16),
            pltpu.VMEM((512, 4 * HID), BF16),
            pltpu.VMEM((4 * HID, HID), BF16),
            pltpu.VMEM((HID, D), BF16),
            pltpu.VMEM((DEVICES, HID, FEAT), F32),
            pltpu.VMEM((DEVICES, ROWS, FEAT), BF16),
            pltpu.VMEM((HALF[0], HID), BF16),
            pltpu.VMEM((HALF[1], HID), BF16),
            pltpu.VMEM((HALF[0], HID), BF16),
            pltpu.VMEM((HALF[1], HID), BF16),
            pltpu.VMEM((DEVICES, HALF[0], HID), BF16),
            pltpu.VMEM((DEVICES, HALF[1], HID), BF16),
            pltpu.VMEM((DEVICES, WIDE, FEAT), BF16),
            pltpu.VMEM((ROWS, FEAT), F32),
            *halves,
            pltpu.VMEM((HALF[0], HID), F32),
            pltpu.VMEM((HALF[1], HID), F32),
            pltpu.VMEM((QROWS, HID), BF16),
            pltpu.VMEM((128, 512), F32),
            pltpu.VMEM((2, 512, 128), BF16),
            pltpu.VMEM((512, 128), F32),
            pltpu.VMEM((2, HID, QROWS), F32),
            pltpu.VMEM((HID, 2 * SIDE * FEAT), BF16),
            pltpu.VMEM((2, 8, 128), F32),
            pltpu.VMEM((10, 8, 128), F32),
            pltpu.VMEM((2, 8, 128), F32),
            pltpu.VMEM((10, 8, 128), F32),
            dma((9,)),
            *gather_sems * 4,
            dma((12,)),
            dma((8,)),
            dma((8,)),
            dma((8,)),
            dma((8,)),
            dma((14,)),
            dma((14,)),
            dma((10,)),
            dma((10,)),
            dma((10,)),
            dma((10,)),
        ],
        compiler_params=pltpu.CompilerParams(
            collective_id=0, has_side_effects=True, vmem_limit_bytes=60 * 1024 * 1024
        ),
    )(activations, out_grads, valid_counts, basis_in, basis_out.T, eigvals, query_out, query_in)
    return jnp.sum(summed.reshape(2, PLANES, RANK), axis=2)


def solution(mesh):
    in_specs = (
        P("grp", None, "mp"),
        P("grp", None, "mp"),
        P("grp"),
        P(None, "mp"),
        P("grp", "mp"),
        P("mp", None),
        P("grp", None, "mp"),
        P("grp", None, "mp"),
    )
    return jax.shard_map(
        per_device, mesh=mesh, in_specs=in_specs, out_specs=P("grp", None), check_vma=False
    )
```

```python
import functools

import jax
import jax.numpy as jnp
from jax import lax
from jax.experimental import pallas as pl
from jax.experimental.pallas import tpu as pltpu
from jax.sharding import PartitionSpec as P

MESH = pl.DeviceIdType.MESH
F32 = jnp.float32
BF16 = jnp.bfloat16

SIDE = 4
PLANES = 8
DEVICES = 32
TOKENS = 192
RANK = 16
ROWS = TOKENS + RANK
LEN = 96
HID = 448
FEAT = 256
QROWS = PLANES * RANK
WIDE = TOKENS + QROWS
FF = HID * DEVICES
D = FEAT * DEVICES


def mod(value, n):
    return lax.rem(value + 2 * n, n)


BOTH = (1, -1)
RING = (
    ((0, 0), BOTH, BOTH),
    ((-1, 0), (1,), BOTH),
    ((1, 0), (), BOTH),
    ((0, -1), (), (1,)),
    ((0, 1), (), ()),
    ((2, 0), (), BOTH),
    ((-1, -1), (), ()),
    ((-1, 1), (), (-1,)),
    ((1, -1), (), ()),
    ((1, 1), (), (-1,)),
    ((2, -1), (), (1,)),
    ((2, 1), (), ()),
    ((0, 2), (), ()),
    ((-1, 2), (), ()),
    ((1, 2), (), ()),
    ((2, 2), (), ()),
)
EARLY = (((0, 0), (1, -1, 2), BOTH), ((-1, 0), (), BOTH)) + RING[2:]
GROUPS = (0, -1, 1, 2)


def slot_of(x, y, core, d1, d2):
    a = mod(x * (1 - core) + y * core + d1, SIDE)
    b = mod(y * (1 - core) + x * core + d2, SIDE)
    return ((a * (1 - core) + b * core) * SIDE + b * (1 - core) + a * core) * 2 + core


class Gather:
    def __init__(self, place, buf, send_sems, recv_sems):
        self.z, self.m, self.x, self.y, self.core = place
        self.buf, self.send_sems, self.recv_sems = buf, send_sems, recv_sems
        self.sibling = self.m + 1 - 2 * self.core
        self.sent = []

    def slot(self, d1, d2):
        return slot_of(self.x, self.y, self.core, d1, d2)

    def copy(self, slot, to, index):
        return pltpu.make_async_remote_copy(
            src_ref=self.buf.at[slot],
            dst_ref=self.buf.at[slot],
            send_sem=self.send_sems.at[index],
            recv_sem=self.recv_sems.at[slot],
            device_id=(self.z, to),
            device_id_type=MESH,
        )

    def send(self, slot, to):
        copy = self.copy(slot, to, len(self.sent))
        copy.start()
        self.sent.append(copy)

    def arrive(self, slot):
        self.copy(slot, self.sibling, 0).wait_recv()

    def event(self, offset, first=(), second=()):
        slot = self.slot(*offset)
        if offset != (0, 0):
            self.arrive(slot)
        for step in first:
            self.send(slot, self.slot(step, 0))
        for step in second:
            self.send(slot, self.slot(0, step))
        self.send(slot, self.sibling)

    def events(self, plan):
        return [functools.partial(self.event, *entry) for entry in plan]

    def group(self, d1):
        def body(d2, carry):
            self.arrive(slot_of(self.x, self.y, 1 - self.core, d1, d2))
            return carry

        lax.fori_loop(0, SIDE, body, 0)

    def rest(self):
        def body(chip, carry):
            self.arrive(chip * 2 + 1 - self.core)
            return carry

        lax.fori_loop(0, SIDE * SIDE, body, 0)

    def finish(self):
        for copy in self.sent:
            copy.wait_send()


def plane_sum(place, tiles, landed, send_sems, recv_sems):
    z = place[0]
    row, column = sum_peers(place)
    sent = []

    def exchange(stage, base, peers):
        for index, peer in enumerate(peers):
            copy = pltpu.make_async_remote_copy(
                src_ref=tiles.at[stage],
                dst_ref=landed.at[base + index],
                send_sem=send_sems.at[base + index],
                recv_sem=recv_sems.at[base + index],
                device_id=(z, peer),
                device_id_type=MESH,
            )
            copy.start()
            sent.append(copy)

    def collect(stage, base, peers):
        total = tiles[stage]
        for index in range(len(peers)):
            sent[base + index].wait_recv()
            total = total + landed[base + index]
        return total

    def first():
        exchange(0, 0, row)

    def second():
        tiles[1] = collect(0, 0, row)
        exchange(1, len(row), column)

    def last():
        return collect(1, len(row), column)

    return first, second, last, sent


def sum_peers(place):
    z, m, x, y, core = place
    row = []
    for ox in range(SIDE):
        for oc in range(2):
            if ox or oc:
                row.append((mod(x + ox, SIDE) * SIDE + y) * 2 + lax.rem(core + oc, 2))
    column = [(x * SIDE + mod(y + o, SIDE)) * 2 + core for o in (1, 2, 3)]
    return row, column


PLAN_A, PLAN_G, PLAN_W = RING, EARLY, RING
SCHEDULE = (
    "sG", "sH", "sI", "sJ", "A0", "turn", "eig", "rG", "rH", "rI", "rJ", "A1", "A2", "A3",
    "A4", "eig2", "tG", "G0", "A5", "tH", "H0", "A7", "A6", "A9", "tI", "I0", "G2", "A8", "G4",
    "A12", "damp", "inv0", "G1", "H2", "G3", "G5", "A11", "H4", "tJ", "J0", "A10", "rot0",
    "H1", "H5", "A13", "H3", "A14", "inv1", "I1", "I2", "I3", "I4", "I5", "G8", "G9", "G6",
    "rot1", "G7", "H8", "H9", "G12", "G11", "rot2", "G10", "J2", "J1", "inv2", "J4", "J5",
    "J3", "H7", "inv3", "H11", "A15", "I7", "H6", "I9", "H10", "I11", "H12", "G14", "I6",
    "rot3", "G13", "H14", "I8", "rotd", "G15", "J7", "J9", "I10", "J8", "J11", "I12", "H13",
    "J6", "zG0", "pG1", "J10", "J12", "I13", "I14", "H15", "W0", "J13", "I15", "J14", "zH0",
    "pH1", "zG1", "pG2", "zI0", "pI1", "J15", "W1", "W2", "zH1", "pH2", "zJ0", "zG2", "pG3",
    "pJ1", "zI1", "pI2", "W3", "W4", "W5", "W7", "zH2", "pH3", "W6", "W9", "zJ1", "pJ2", "W8",
    "zG3", "zI2", "pI3", "W11", "W12", "zH3", "W13", "W10", "zJ2", "pJ3", "zG4", "W14", "zI3",
    "zH4", "sc00", "sc01", "zJ3", "W15", "zI4", "sc02", "sc03", "zJ4", "sc10", "sc11", "sc12",
    "qt", "sc13",
)
PART = LEN // 2
CHUNKS = (PART, PART, PART, PART + RANK)
SUMMED = (PART, PART, PART, PART + 2 * RANK)
LETTERS = "GHIJ"


def kernel(
    acts,
    grads,
    counts,
    basis_in,
    basis_out,
    eigvals,
    query_out,
    query_in,
    out,
    *scratch,
):
    names = iter(scratch)
    bin_v, bout_t, bout_v, eig_v, inverse, acts_all, wide_all, acc_in = (next(names) for _ in range(8))
    qout_all, pad, left, qout_t, mixed, weighted = (next(names) for _ in range(6))
    tiles1, landed1, tiles2, landed2 = (next(names) for _ in range(4))
    stage, relay, grads_all, kept_a, kept_b, landed_a, landed_b, mine = (
        [next(names) for _ in CHUNKS] for _ in range(8)
    )
    local_sems, perm_sems, qin_send, qin_recv, qout_send, qout_recv = (next(names) for _ in range(6))
    z_send, z_recv, sum1_send, sum1_recv, sum2_send, sum2_recv = (next(names) for _ in range(6))
    gather_sems = [(next(names), next(names)) for _ in range(6)]

    z = lax.axis_index("grp")
    m = lax.axis_index("mp")
    core = lax.rem(m, 2)
    chip = lax.div(m, 2)
    x, y = lax.div(chip, SIDE), lax.rem(chip, SIDE)
    place = (z, m, x, y, core)

    y_low, y_high = lax.rem(y, 2), lax.div(y, 2)

    def place_of(target, j_high, j_low, source):
        ring = mod(target - source - 4 * j_low, PLANES)
        high = lax.rem(ring, 2)
        low = lax.rem(j_high + lax.rem(target, 2) + high, 2)
        return (lax.div(ring, 2) * SIDE + 2 * high + low) * 2 + j_low

    x_relay = lax.div(mod(2 * x + y_high - z - 4 * core, PLANES), 2)
    relay_to = (x_relay * SIDE + y) * 2 + core
    ring = 2 * x + lax.rem(y_high + z, 2)
    plane = lax.rem(ring + z + 4 * core, PLANES)
    to = place_of(plane, y_low, core, z)
    from_plane = mod(z - (2 * x + y_high) - 4 * core, PLANES)
    from_y = 2 * lax.rem(z, 2) + lax.rem(y_low + y_high + lax.rem(z, 2), 2)
    from_device = (x * SIDE + from_y) * 2 + core
    shifts = x_relay != x
    stays = jnp.logical_and(plane == z, to == m)
    moves = jnp.logical_not(stays)

    barrier = pltpu.get_barrier_semaphore()
    row, column = sum_peers(place)
    for peer in row + column:
        pl.semaphore_signal(barrier, inc=1, device_id=(z, peer), device_id_type=MESH)
    for o in range(1, PLANES):
        pl.semaphore_signal(
            barrier, inc=1, device_id=(mod(z + o, PLANES), m), device_id_type=MESH
        )

    @pl.when(moves)
    def _():
        pl.semaphore_signal(
            barrier, inc=1, device_id=(from_plane, from_device), device_id_type=MESH
        )

    loads = []

    def load(src, dst):
        copy = pltpu.make_async_copy(src, dst, local_sems.at[len(loads)])
        copy.start()
        loads.append(copy)

    for h in range(len(CHUNKS)):
        rows = pl.ds(h % 2 * PART, PART)
        load(grads.at[h // 2, rows], stage[h].at[pl.ds(0, PART)])
    load(query_out.at[0], stage[-1].at[pl.ds(PART, RANK)])
    load(acts.at[0], acts_all.at[m, pl.ds(0, LEN)])
    load(acts.at[1], acts_all.at[m, pl.ds(LEN, LEN)])
    load(query_in.at[0], acts_all.at[m, pl.ds(TOKENS, RANK)])
    first_loads = list(loads)
    load(eigvals, eig_v)
    load(basis_out, bout_t.at[pl.ds(0, HID)])
    load(basis_in, bin_v)
    load_eig, load_out, load_in = loads[-3:]

    pl.semaphore_wait(
        barrier, len(row) + len(column) + PLANES - 1 + jnp.where(stays, 0, 1)
    )

    shift, shift_here, permute, permute_here = [], [], [], []
    chunks = len(CHUNKS)
    for h in range(chunks):
        shift.append(
            pltpu.make_async_remote_copy(
                src_ref=stage[h],
                dst_ref=relay[h],
                send_sem=perm_sems.at[0, h],
                recv_sem=perm_sems.at[1, h],
                device_id=(z, relay_to),
                device_id_type=MESH,
            )
        )
        shift_here.append(pltpu.make_async_copy(stage[h], relay[h], perm_sems.at[2, h]))
        permute.append(
            pltpu.make_async_remote_copy(
                src_ref=relay[h],
                dst_ref=grads_all[h].at[to],
                send_sem=perm_sems.at[3, h],
                recv_sem=perm_sems.at[4, h],
                device_id=(plane, to),
                device_id_type=MESH,
            )
        )
        permute_here.append(
            pltpu.make_async_copy(relay[h], grads_all[h].at[m], perm_sems.at[5, h])
        )

    def one_of(predicate, yes, no):
        @pl.when(predicate)
        def _():
            yes()

        @pl.when(jnp.logical_not(predicate))
        def _():
            no()

    for copy in first_loads:
        copy.wait()
    gather_acts = Gather(place, acts_all, *gather_sems[0])
    gather_wide = Gather(place, wide_all, *gather_sems[1])
    gather_grads = [Gather(place, grads_all[h], *gather_sems[2 + h]) for h in range(chunks)]
    run = {}
    for letter, gather, plan in (
        ("A", gather_acts, PLAN_A),
        ("W", gather_wide, PLAN_W),
        *((letter, gather, PLAN_G) for letter, gather in zip(LETTERS, gather_grads)),
    ):
        for index, event in enumerate(gather.events(plan)):
            run[letter + str(index)] = event

    def relay_block(h):
        one_of(shifts, shift[h].wait, shift_here[h].wait)
        one_of(moves, permute[h].start, permute_here[h].start)

    def take_block(h):
        one_of(moves, permute[h].wait, permute_here[h].wait)

    sum_first, sum_second, sum_last, sum1_sent = plane_sum(
        place, tiles1, landed1, sum1_send, sum1_recv
    )

    def sum_eig():
        load_eig.wait()

        def add_eig(slot, total):
            columns = pl.ds(pl.multiple_of(slot * FEAT, FEAT), FEAT)
            block = eig_v[:, columns].astype(F32).reshape(HID // 8, 8, FEAT)
            return total + jnp.sum(block, axis=0)

        eig_sum = lax.fori_loop(0, DEVICES, add_eig, jnp.zeros((8, FEAT), F32))
        tiles1[0] = eig_sum[:, :128] + eig_sum[:, 128:]
        sum_first()

    def turn_basis():
        load_out.wait()

        def turn(i, carry):
            rows = pl.ds(pl.multiple_of(i * 128, 128), 128)
            turned = bout_t[:, rows].astype(F32).T
            bout_v[rows, :] = turned[:, :HID].astype(BF16)
            return carry

        lax.fori_loop(0, 4 * HID // 128, turn, 0)

    def invert(start, stop):
        def body(slot, carry):
            columns = pl.ds(pl.multiple_of(slot * FEAT, FEAT), FEAT)
            inverse[slot] = 1.0 / (eig_v[:, columns].astype(F32) + scale[0])
            return carry

        lax.fori_loop(start, stop, body, 0)

    qin_sent = []
    my_query = pl.ds(pl.multiple_of(TOKENS + z * RANK, RANK), RANK)

    def group_slots(group):
        return [
            slot_of(x, y, lax.rem(core + k, 2), GROUPS[group], k // 2) for k in range(2 * SIDE)
        ]

    def rotate_group(group):
        gather_acts.group(GROUPS[group])
        if group == 0:
            load_in.wait()
            acc_in[...] = jnp.zeros_like(acc_in)

        total = None
        for slot in group_slots(group):
            rows = pl.ds(pl.multiple_of(slot * FEAT, FEAT), FEAT)
            term = jnp.dot(acts_all[slot], bin_v[rows, :], preferred_element_type=F32)
            total = term if total is None else total + term
        acc_in[...] += total

    def rotated():
        position = lax.broadcasted_iota(jnp.int32, (LEN, FEAT), 0)
        for s in range(2):
            rows = pl.ds(s * LEN, LEN)
            kept = jnp.where(position < counts[s], acc_in[rows, :], 0.0)
            wide_all[m, rows, :] = kept.astype(BF16)
        wide_all[m, my_query, :] = acc_in[pl.ds(TOKENS, RANK), :].astype(BF16)
        for o in range(1, PLANES):
            copy = pltpu.make_async_remote_copy(
                src_ref=wide_all.at[m, my_query],
                dst_ref=wide_all.at[m, my_query],
                send_sem=qin_send.at[o],
                recv_sem=qin_recv.at[o],
                device_id=(mod(z + o, PLANES), m),
                device_id_type=MESH,
            )
            copy.start()
            qin_sent.append(copy)

    toward = 1 - 2 * core
    ahead = mod(z + toward, PLANES)
    behind = mod(z - toward, PLANES)
    z_sent = []
    last = {}

    def pair(h, offsets):
        total = None
        slots = [mod(z + toward * offset, PLANES) for offset in offsets]
        for j in range(4):
            lhs = [grads_all[h][place_of(z, j // 2, j % 2, source)] for source in slots]
            term = jnp.dot(
                jnp.concatenate(lhs, axis=0),
                bout_v[pl.ds(j * HID, HID), :],
                preferred_element_type=F32,
            )
            total = term if total is None else total + term
        return total[: CHUNKS[h]], total[CHUNKS[h] :]

    def hop(h, way, step):
        index = h * 7 + way * 4 + step
        copy = pltpu.make_async_remote_copy(
            src_ref=(kept_a, kept_b)[way][h].at[step],
            dst_ref=(landed_a, landed_b)[way][h].at[step],
            send_sem=z_send.at[index],
            recv_sem=z_recv.at[index],
            device_id=((ahead, behind)[way], m),
            device_id_type=MESH,
        )
        copy.start()
        z_sent.append(copy)
        last[h, way] = copy

    products = {}
    turned = set()

    def product(h, step):
        products[h] = pair(h, ((4, -3), (3, -2), (2, -1), (1, 0))[step])

    def keep(ref, step, value):
        tokens = value[:PART].astype(BF16)
        ref[step, pl.ds(0, PART), :] = tokens
        if value.shape[0] > PART:
            high = value[PART:].astype(BF16)
            ref[step, pl.ds(PART, RANK), :] = high
            ref[step, pl.ds(PART + RANK, RANK), :] = (value[PART:] - high.astype(F32)).astype(BF16)

    def landed(ref, step):
        value = ref[step].astype(F32)
        if value.shape[0] == PART:
            return value
        query = value[PART : PART + RANK] + value[PART + RANK :]
        return jnp.concatenate([value[:PART], query], axis=0)

    def reduce_step(h, step):
        if step == 0:
            gather_grads[h].rest()
            product(h, 0)
            a, b = products[h]
            keep(kept_a[h], 0, a)
            hop(h, 0, 0)
            keep(kept_b[h], 0, b)
            hop(h, 1, 0)
        elif step < 4:
            a, b = products[h]
            last[h, 0].wait_recv()
            keep(kept_a[h], step, a + landed(landed_a[h], step - 1))
            hop(h, 0, step)
            last[h, 1].wait_recv()
            b = b + landed(landed_b[h], step - 1)
            if step < 3:
                keep(kept_b[h], step, b)
                hop(h, 1, step)
            else:
                mine[h][...] = b
        else:
            last[h, 0].wait_recv()
            value = mine[h][...] + landed(landed_a[h], 3)
            s = h // 2
            pad[s, pl.ds(h % 2 * PART, PART), pl.ds(0, HID)] = value[:PART]
            if s in turned:
                left[s] = pad[s].T.astype(BF16)
            turned.add(s)
            if h == chunks - 1:
                send_qout(value[PART:])

    my_rows = pl.ds(pl.multiple_of(z * RANK, RANK), RANK)
    qout_sent = []

    def send_qout(rotated_query):
        qout_all[my_rows, :] = rotated_query.astype(BF16)
        for o in range(1, PLANES):
            copy = pltpu.make_async_remote_copy(
                src_ref=qout_all.at[my_rows],
                dst_ref=qout_all.at[my_rows],
                send_sem=qout_send.at[o],
                recv_sem=qout_recv.at[o],
                device_id=(mod(z + o, PLANES), m),
                device_id_type=MESH,
            )
            copy.start()
            qout_sent.append(copy)

    arrived = set()

    def score(s, group):
        if group not in arrived:
            arrived.add(group)
            gather_wide.group(GROUPS[group])

        slots = group_slots(group)
        for k, slot in enumerate(slots):
            outer = jnp.dot(
                left[s, pl.ds(0, HID), :],
                wide_all[slot, pl.ds(s * LEN, 128), :],
                preferred_element_type=F32,
            )
            weighted[:, pl.ds(k * FEAT, FEAT)] = (outer * inverse[slot]).astype(BF16)
        queries = [wide_all[slot, pl.ds(TOKENS, QROWS), :] for slot in slots]
        mixed[s] += lax.dot_general(
            weighted[...],
            jnp.concatenate(queries, axis=1),
            (((1,), (1,)), ((), ())),
            preferred_element_type=F32,
        )

    def turn_queries():
        for copy in qout_sent:
            copy.wait_recv()
        pad[2, :, pl.ds(0, HID)] = qout_all[...].astype(F32)
        qout_t[...] = pad[2].T

    def start_wide():
        for copy in qin_sent:
            copy.wait_recv()
        run["W"]()

    scale = []

    def damp():
        scale.append(0.1 * jnp.sum(sum_last()) / (FF * D))

    run["W"], run["W0"] = run["W0"], start_wide
    for h, letter in enumerate(LETTERS):
        run["s" + letter] = functools.partial(one_of, shifts, shift[h].start, shift_here[h].start)
        run["r" + letter] = functools.partial(relay_block, h)
        run["t" + letter] = functools.partial(take_block, h)
        for step in range(5):
            run["z" + letter + str(step)] = functools.partial(reduce_step, h, step)
            run["p" + letter + str(step)] = functools.partial(product, h, step)
    for group in range(SIDE):
        run["rot" + str(group)] = functools.partial(rotate_group, group)
        run["inv" + str(group)] = functools.partial(invert, 8 * group, 8 * group + 8)
        for s in range(2):
            run["sc" + str(s) + str(group)] = functools.partial(score, s, group)
    run.update(eig=sum_eig, eig2=sum_second, turn=turn_basis, damp=damp, qt=turn_queries, rotd=rotated)

    pad[...] = jnp.zeros_like(pad)
    mixed[...] = jnp.zeros_like(mixed)
    for name in SCHEDULE:
        run[name]()

    tiles2[0] = jnp.zeros((8, 128), F32)
    for s in range(2):
        tiles2[0, pl.ds(s, 1), :] = jnp.sum(
            mixed[s] * qout_t[pl.ds(0, HID), :], axis=0, keepdims=True
        )
    end_first, end_second, end_last, sum2_sent = plane_sum(
        place, tiles2, landed2, sum2_send, sum2_recv
    )
    end_first()
    end_second()
    out[...] = end_last()[:2]

    for gather in (gather_acts, *gather_grads, gather_wide):
        gather.finish()
    for copy in qin_sent + qout_sent + z_sent + sum1_sent + sum2_sent:
        copy.wait_send()


def per_device(
    activations, out_grads, valid_counts, basis_in, basis_out, eigvals, query_out, query_in
):
    anywhere = pl.BlockSpec(memory_space=pl.ANY)
    dma = pltpu.SemaphoreType.DMA
    vmem = pltpu.VMEM
    per_chunk = [[vmem((rows, HID), BF16) for rows in CHUNKS]] * 2
    per_chunk.append([vmem((DEVICES, rows, HID), BF16) for rows in CHUNKS])
    per_chunk += [[vmem((steps, rows, HID), BF16) for rows in SUMMED] for steps in (4, 3, 4, 3)]
    per_chunk.append([vmem((rows, HID), F32) for rows in CHUNKS])
    summed = pl.pallas_call(
        kernel,
        out_shape=jax.ShapeDtypeStruct((2, 128), F32),
        in_specs=[anywhere, anywhere, pl.BlockSpec(memory_space=pltpu.SMEM)] + [anywhere] * 5,
        out_specs=pl.BlockSpec(memory_space=pltpu.VMEM),
        scratch_shapes=[
            vmem((D, FEAT), BF16),
            vmem((512, 4 * HID), BF16),
            vmem((4 * HID, HID), BF16),
            vmem((HID, D), BF16),
            vmem((DEVICES, HID, FEAT), F32),
            vmem((DEVICES, ROWS, FEAT), BF16),
            vmem((DEVICES, WIDE, FEAT), BF16),
            vmem((ROWS, FEAT), F32),
            vmem((QROWS, HID), BF16),
            vmem((3, 128, 512), F32),
            vmem((2, 512, 128), BF16),
            vmem((512, 128), F32),
            vmem((2, HID, QROWS), F32),
            vmem((HID, 2 * SIDE * FEAT), BF16),
            vmem((2, 8, 128), F32),
            vmem((10, 8, 128), F32),
            vmem((2, 8, 128), F32),
            vmem((10, 8, 128), F32),
            *sum(per_chunk, []),
            dma((11,)),
            dma((6, len(CHUNKS))),
            *[dma((PLANES,))] * 4,
            *[dma((7 * len(CHUNKS),))] * 2,
            *[dma((10,))] * 4,
            *[dma((31,)), dma((32,))] * (2 + len(CHUNKS)),
        ],
        compiler_params=pltpu.CompilerParams(
            collective_id=0, has_side_effects=True, vmem_limit_bytes=60 * 1024 * 1024
        ),
    )(activations, out_grads, valid_counts, basis_in, basis_out.T, eigvals, query_out, query_in)
    return jnp.sum(summed.reshape(2, PLANES, RANK), axis=2)


def solution(mesh):
    in_specs = (
        P("grp", None, "mp"),
        P("grp", None, "mp"),
        P("grp"),
        P(None, "mp"),
        P("grp", "mp"),
        P("mp", None),
        P("grp", None, "mp"),
        P("grp", None, "mp"),
    )
    return jax.shard_map(
        per_device, mesh=mesh, in_specs=in_specs, out_specs=P("grp", None), check_vma=False
    )
```

```python
import functools

import jax
import jax.numpy as jnp
from jax import lax
from jax.experimental import pallas as pl
from jax.experimental.pallas import tpu as pltpu
from jax.sharding import PartitionSpec as P

MESH = pl.DeviceIdType.MESH
F32 = jnp.float32
BF16 = jnp.bfloat16

SIDE = 4
PLANES = 8
DEVICES = 32
TOKENS = 192
RANK = 16
ROWS = TOKENS + RANK
LEN = 96
HID = 448
FEAT = 256
QROWS = PLANES * RANK
WIDE = TOKENS + QROWS
FF = HID * DEVICES
D = FEAT * DEVICES


def mod(value, n):
    return lax.rem(value + 2 * n, n)


BOTH = (1, -1)
RING = (
    ((0, 0), BOTH, BOTH),
    ((-1, 0), (1,), BOTH),
    ((1, 0), (), BOTH),
    ((0, -1), (), (1,)),
    ((0, 1), (), ()),
    ((2, 0), (), BOTH),
    ((-1, -1), (), ()),
    ((-1, 1), (), (-1,)),
    ((1, -1), (), ()),
    ((1, 1), (), (-1,)),
    ((2, -1), (), (1,)),
    ((2, 1), (), ()),
    ((0, 2), (), ()),
    ((-1, 2), (), ()),
    ((1, 2), (), ()),
    ((2, 2), (), ()),
)
EARLY = (((0, 0), (1, -1, 2), BOTH), ((-1, 0), (), BOTH)) + RING[2:]
ALL = (1, -1, 2)
DIRECT = (((0, 0), ALL, ALL),) + tuple(((d1, 0), (), ALL) for d1 in (-1, 1, 2))
DIRECT += tuple(((d1, d2), (), ()) for d1 in (0, -1, 1, 2) for d2 in (-1, 1, 2))
GROUPS = (0, -1, 1, 2)


def slot_of(x, y, core, d1, d2):
    a = mod(x * (1 - core) + y * core + d1, SIDE)
    b = mod(y * (1 - core) + x * core + d2, SIDE)
    return ((a * (1 - core) + b * core) * SIDE + b * (1 - core) + a * core) * 2 + core


class Gather:
    def __init__(self, place, buf, send_sems, recv_sems):
        self.z, self.m, self.x, self.y, self.core = place
        self.buf, self.send_sems, self.recv_sems = buf, send_sems, recv_sems
        self.sibling = self.m + 1 - 2 * self.core
        self.sent = []

    def slot(self, d1, d2):
        return slot_of(self.x, self.y, self.core, d1, d2)

    def copy(self, slot, to, index):
        return pltpu.make_async_remote_copy(
            src_ref=self.buf.at[slot],
            dst_ref=self.buf.at[slot],
            send_sem=self.send_sems.at[index],
            recv_sem=self.recv_sems.at[slot],
            device_id=(self.z, to),
            device_id_type=MESH,
        )

    def send(self, slot, to):
        copy = self.copy(slot, to, len(self.sent))
        copy.start()
        self.sent.append(copy)

    def arrive(self, slot):
        self.copy(slot, self.sibling, 0).wait_recv()

    def event(self, offset, first=(), second=()):
        slot = self.slot(*offset)
        if offset != (0, 0):
            self.arrive(slot)
        for step in first:
            self.send(slot, self.slot(step, 0))
        for step in second:
            self.send(slot, self.slot(0, step))
        self.send(slot, self.sibling)

    def events(self, plan):
        return [functools.partial(self.event, *entry) for entry in plan]

    def group(self, d1):
        def body(d2, carry):
            self.arrive(slot_of(self.x, self.y, 1 - self.core, d1, d2))
            return carry

        lax.fori_loop(0, SIDE, body, 0)

    def rest(self):
        def body(chip, carry):
            self.arrive(chip * 2 + 1 - self.core)
            return carry

        lax.fori_loop(0, SIDE * SIDE, body, 0)

    def finish(self):
        for copy in self.sent:
            copy.wait_send()


def plane_sum(place, tiles, landed, send_sems, recv_sems):
    z = place[0]
    row, column = sum_peers(place)
    sent = []

    def exchange(stage, base, peers):
        for index, peer in enumerate(peers):
            copy = pltpu.make_async_remote_copy(
                src_ref=tiles.at[stage],
                dst_ref=landed.at[base + index],
                send_sem=send_sems.at[base + index],
                recv_sem=recv_sems.at[base + index],
                device_id=(z, peer),
                device_id_type=MESH,
            )
            copy.start()
            sent.append(copy)

    def collect(stage, base, peers):
        total = tiles[stage]
        for index in range(len(peers)):
            sent[base + index].wait_recv()
            total = total + landed[base + index]
        return total

    def first():
        exchange(0, 0, row)

    def second():
        tiles[1] = collect(0, 0, row)
        exchange(1, len(row), column)

    def last():
        return collect(1, len(row), column)

    return first, second, last, sent


def sum_peers(place):
    z, m, x, y, core = place
    row = []
    for ox in range(SIDE):
        for oc in range(2):
            if ox or oc:
                row.append((mod(x + ox, SIDE) * SIDE + y) * 2 + lax.rem(core + oc, 2))
    column = [(x * SIDE + mod(y + o, SIDE)) * 2 + core for o in (1, 2, 3)]
    return row, column


PLAN_A, PLAN_G, PLAN_W = EARLY, EARLY, RING
SCHEDULE = (
    "sG", "sH", "sI", "sJ", "A0", "turn", "eig", "rG", "rH", "rI", "rJ", "A1", "A2", "A5",
    "A3", "A4", "eig2", "tG", "G0", "A6", "A7", "A8", "A9", "tI", "I0", "A10", "A11", "G2",
    "A12", "damp", "inv0", "G1", "G4", "G5", "rot0", "G3", "A13", "tH", "H0", "I1", "inv1",
    "A14", "I2", "I3", "I5", "tJ", "J0", "A15", "I4", "rot1", "G8", "G9", "rot2", "G6", "G7",
    "rot3", "G10", "G11", "H2", "G12", "rotd", "H1", "H3", "H4", "H5", "I6", "I7", "I8", "I9",
    "I11", "I12", "J2", "I10", "J1", "G14", "J4", "J3", "J5", "G13", "H9", "G15", "H7", "H8",
    "H11", "H6", "inv2", "H10", "H12", "zG0", "pG1", "I13", "I14", "H14", "H13", "I15", "J6",
    "J7", "J8", "J9", "J10", "J11", "H15", "W0", "zI0", "pI1", "zH0", "pH1", "zG1", "pG2",
    "J12", "J13", "J14", "J15", "inv3", "W1", "W2", "zI1", "pI2", "zH1", "pH2", "zJ0", "pJ1",
    "W3", "W4", "zG2", "pG3", "W5", "zI2", "pI3", "zH2", "pH3", "zJ1", "pJ2", "W6", "W7", "W9",
    "zG3", "W8", "zI3", "W11", "W12", "zH3", "zJ2", "pJ3", "W13", "W10", "zG4", "zI4", "W14",
    "zH4", "sc00", "zJ3", "sc01", "qt", "W15", "sc02", "zJ4", "sc10", "sc03", "sc11", "sc12",
    "sc13",
)
PARTS = ((0, 0, 64), (0, 64, 32), (1, 0, 64), (1, 64, 32))
CHUNKS = tuple(rows + RANK * (h == 0) for h, (_, _, rows) in enumerate(PARTS))
PACKED = tuple(rows * 7 // 2 + 4 * RANK * (h == 0) for h, (_, _, rows) in enumerate(PARTS))
SUMMED = tuple(rows * 7 // 2 + 8 * RANK * (h == 0) for h, (_, _, rows) in enumerate(PARTS))
HALF_LANES = 64
LETTERS = "GHIJ"


def pack(ref, rows, value, at=()):
    value = value.astype(F32)
    for t in range(3):
        ref[(*at, pl.ds(t * rows, rows), slice(None))] = value[:, t * 128 : t * 128 + 128].astype(BF16)
    half = rows // 2
    first, second = value[:half, 384:], value[half:, 384:]
    lane = lax.broadcasted_iota(jnp.int32, (half, 128), 1)
    folded = jnp.where(lane < HALF_LANES, first, pltpu.roll(second, HALF_LANES, 1))
    ref[(*at, pl.ds(3 * rows, half), slice(None))] = folded.astype(BF16)


def unpack(value, rows, kind):
    tiles = [value[t * rows : t * rows + rows].astype(kind) for t in range(3)]
    folded = value[3 * rows : 3 * rows + rows // 2].astype(F32)
    last = jnp.concatenate([folded, pltpu.roll(folded, HALF_LANES, 1)], axis=0)
    return jnp.concatenate([*tiles, last.astype(kind)], axis=1)


def pack_query(ref, start, value, at=()):
    lane = lax.broadcasted_iota(jnp.int32, (RANK, 128), 1)
    for t in range(4):
        tile = value[:, t * 128 : t * 128 + 128].astype(F32)
        if t == 3:
            tile = jnp.where(lane < HALF_LANES, tile, 0.0)
        ref[(*at, pl.ds(start + t * RANK, RANK), slice(None))] = tile.astype(BF16)


def unpack_query(value, start, kind):
    tiles = [value[start + t * RANK : start + t * RANK + RANK] for t in range(4)]
    return jnp.concatenate(tiles, axis=1).astype(kind)


def kernel(
    acts,
    grads,
    counts,
    basis_in,
    basis_out,
    eigvals,
    query_out,
    query_in,
    out,
    *scratch,
):
    names = iter(scratch)
    bin_v, bout_t, bout_v, eig_v, inverse, acts_all, wide_all, acc_in = (next(names) for _ in range(8))
    qout_all, pad, left, qout_t, mixed, weighted = (next(names) for _ in range(6))
    tiles1, landed1, tiles2, landed2 = (next(names) for _ in range(4))
    raw, stage, relay, grads_all, kept_a, kept_b, landed_a, landed_b, mine = (
        [next(names) for _ in CHUNKS] for _ in range(9)
    )
    local_sems, perm_sems, qin_send, qin_recv, qout_send, qout_recv = (next(names) for _ in range(6))
    z_send, z_recv, sum1_send, sum1_recv, sum2_send, sum2_recv = (next(names) for _ in range(6))
    gather_sems = [(next(names), next(names)) for _ in range(6)]

    z = lax.axis_index("grp")
    m = lax.axis_index("mp")
    core = lax.rem(m, 2)
    chip = lax.div(m, 2)
    x, y = lax.div(chip, SIDE), lax.rem(chip, SIDE)
    place = (z, m, x, y, core)

    y_low, y_high = lax.rem(y, 2), lax.div(y, 2)

    def place_of(target, j_high, j_low, source):
        ring = mod(target - source - 4 * j_low, PLANES)
        high = lax.rem(ring, 2)
        low = lax.rem(j_high + lax.rem(target, 2) + high, 2)
        return (lax.div(ring, 2) * SIDE + 2 * high + low) * 2 + j_low

    x_relay = lax.div(mod(2 * x + y_high - z - 4 * core, PLANES), 2)
    relay_to = (x_relay * SIDE + y) * 2 + core
    ring = 2 * x + lax.rem(y_high + z, 2)
    plane = lax.rem(ring + z + 4 * core, PLANES)
    to = place_of(plane, y_low, core, z)
    from_plane = mod(z - (2 * x + y_high) - 4 * core, PLANES)
    from_y = 2 * lax.rem(z, 2) + lax.rem(y_low + y_high + lax.rem(z, 2), 2)
    from_device = (x * SIDE + from_y) * 2 + core
    shifts = x_relay != x
    stays = jnp.logical_and(plane == z, to == m)
    moves = jnp.logical_not(stays)

    barrier = pltpu.get_barrier_semaphore()
    row, column = sum_peers(place)
    for peer in row + column:
        pl.semaphore_signal(barrier, inc=1, device_id=(z, peer), device_id_type=MESH)
    for o in range(1, PLANES):
        pl.semaphore_signal(
            barrier, inc=1, device_id=(mod(z + o, PLANES), m), device_id_type=MESH
        )

    @pl.when(moves)
    def _():
        pl.semaphore_signal(
            barrier, inc=1, device_id=(from_plane, from_device), device_id_type=MESH
        )

    loads = []

    def load(src, dst):
        copy = pltpu.make_async_copy(src, dst, local_sems.at[len(loads)])
        copy.start()
        loads.append(copy)

    for h, (s, first, rows) in enumerate(PARTS):
        load(grads.at[s, pl.ds(first, rows)], raw[h].at[pl.ds(0, rows)])
    load(query_out.at[0], raw[0].at[pl.ds(PARTS[0][2], RANK)])
    load(acts.at[0], acts_all.at[m, pl.ds(0, LEN)])
    load(acts.at[1], acts_all.at[m, pl.ds(LEN, LEN)])
    load(query_in.at[0], acts_all.at[m, pl.ds(TOKENS, RANK)])
    first_loads = list(loads)
    load(eigvals, eig_v)
    load(basis_out, bout_t.at[pl.ds(0, HID)])
    load(basis_in, bin_v)
    load_eig, load_out, load_in = loads[-3:]

    pl.semaphore_wait(
        barrier, len(row) + len(column) + PLANES - 1 + jnp.where(stays, 0, 1)
    )

    shift, shift_here, permute, permute_here = [], [], [], []
    chunks = len(CHUNKS)
    for h in range(chunks):
        shift.append(
            pltpu.make_async_remote_copy(
                src_ref=stage[h],
                dst_ref=relay[h],
                send_sem=perm_sems.at[0, h],
                recv_sem=perm_sems.at[1, h],
                device_id=(z, relay_to),
                device_id_type=MESH,
            )
        )
        shift_here.append(pltpu.make_async_copy(stage[h], relay[h], perm_sems.at[2, h]))
        permute.append(
            pltpu.make_async_remote_copy(
                src_ref=relay[h],
                dst_ref=grads_all[h].at[to],
                send_sem=perm_sems.at[3, h],
                recv_sem=perm_sems.at[4, h],
                device_id=(plane, to),
                device_id_type=MESH,
            )
        )
        permute_here.append(
            pltpu.make_async_copy(relay[h], grads_all[h].at[m], perm_sems.at[5, h])
        )

    def one_of(predicate, yes, no):
        @pl.when(predicate)
        def _():
            yes()

        @pl.when(jnp.logical_not(predicate))
        def _():
            no()

    pad[...] = jnp.zeros_like(pad)
    for copy in first_loads:
        copy.wait()
    for h, (_, _, rows) in enumerate(PARTS):
        pad[2, pl.ds(0, CHUNKS[h]), pl.ds(0, HID)] = raw[h][...].astype(F32)
        value = pad[2, pl.ds(0, CHUNKS[h]), :]
        pack(stage[h], rows, value[:rows])
        if h == 0:
            pack_query(stage[h], rows * 7 // 2, value[rows:])
    gather_acts = Gather(place, acts_all, *gather_sems[0])
    gather_wide = Gather(place, wide_all, *gather_sems[1])
    gather_grads = [Gather(place, grads_all[h], *gather_sems[2 + h]) for h in range(chunks)]
    run = {}
    for letter, gather, plan in (
        ("A", gather_acts, PLAN_A),
        ("W", gather_wide, PLAN_W),
        *((letter, gather, PLAN_G) for letter, gather in zip(LETTERS, gather_grads)),
    ):
        for index, event in enumerate(gather.events(plan)):
            run[letter + str(index)] = event

    def relay_block(h):
        one_of(shifts, shift[h].wait, shift_here[h].wait)
        one_of(moves, permute[h].start, permute_here[h].start)

    def take_block(h):
        one_of(moves, permute[h].wait, permute_here[h].wait)

    sum_first, sum_second, sum_last, sum1_sent = plane_sum(
        place, tiles1, landed1, sum1_send, sum1_recv
    )

    def sum_eig():
        load_eig.wait()

        def add_eig(slot, total):
            columns = pl.ds(pl.multiple_of(slot * FEAT, FEAT), FEAT)
            block = eig_v[:, columns].astype(F32).reshape(HID // 8, 8, FEAT)
            return total + jnp.sum(block, axis=0)

        eig_sum = lax.fori_loop(0, DEVICES, add_eig, jnp.zeros((8, FEAT), F32))
        tiles1[0] = eig_sum[:, :128] + eig_sum[:, 128:]
        sum_first()

    def turn_basis():
        load_out.wait()

        bout_t[pl.ds(HID, 512 - HID), :] = jnp.zeros((512 - HID, 4 * HID), BF16)

        def turn(i, carry):
            turned = bout_t[:, pl.ds(pl.multiple_of(i * 128, 128), 128)].astype(F32).T.astype(BF16)
            for k in range(2):
                piece = 2 * i + k
                row = lax.div(piece, 7) * 512 + lax.rem(piece, 7) * HALF_LANES
                rows = pl.ds(pl.multiple_of(row, HALF_LANES), HALF_LANES)
                bout_v[rows, :] = turned[k * HALF_LANES : (k + 1) * HALF_LANES]
            return carry

        lax.fori_loop(0, 4 * HID // 128, turn, 0)
        for j in range(4):
            rows = pl.ds(j * 512 + HID, 512 - HID)
            bout_v[rows, :] = jnp.zeros((512 - HID, 512), BF16)

    def invert(start, stop):
        def body(slot, carry):
            columns = pl.ds(pl.multiple_of(slot * FEAT, FEAT), FEAT)
            inverse[slot] = 1.0 / (eig_v[:, columns].astype(F32) + scale[0])
            return carry

        lax.fori_loop(start, stop, body, 0)

    qin_sent = []
    my_query = pl.ds(pl.multiple_of(TOKENS + z * RANK, RANK), RANK)

    def group_slots(group):
        return [
            slot_of(x, y, lax.rem(core + k, 2), GROUPS[group], k // 2) for k in range(2 * SIDE)
        ]

    def rotate_group(group):
        gather_acts.group(GROUPS[group])
        if group == 0:
            load_in.wait()
            acc_in[...] = jnp.zeros_like(acc_in)

        total = None
        for slot in group_slots(group):
            rows = pl.ds(pl.multiple_of(slot * FEAT, FEAT), FEAT)
            term = jnp.dot(acts_all[slot], bin_v[rows, :], preferred_element_type=F32)
            total = term if total is None else total + term
        acc_in[...] += total

    def rotated():
        position = lax.broadcasted_iota(jnp.int32, (LEN, FEAT), 0)
        for s in range(2):
            rows = pl.ds(s * LEN, LEN)
            kept = jnp.where(position < counts[s], acc_in[rows, :], 0.0)
            wide_all[m, rows, :] = kept.astype(BF16)
        wide_all[m, my_query, :] = acc_in[pl.ds(TOKENS, RANK), :].astype(BF16)
        for o in range(1, PLANES):
            copy = pltpu.make_async_remote_copy(
                src_ref=wide_all.at[m, my_query],
                dst_ref=wide_all.at[m, my_query],
                send_sem=qin_send.at[o],
                recv_sem=qin_recv.at[o],
                device_id=(mod(z + o, PLANES), m),
                device_id_type=MESH,
            )
            copy.start()
            qin_sent.append(copy)

    toward = 1 - 2 * core
    ahead = mod(z + toward, PLANES)
    behind = mod(z - toward, PLANES)
    z_sent = []
    last = {}

    def pair(h, offsets):
        total = None
        slots = [mod(z + toward * offset, PLANES) for offset in offsets]
        for j in range(4):
            lhs = []
            for source in slots:
                block = grads_all[h][place_of(z, j // 2, j % 2, source)]
                lhs.append(unpack(block, PARTS[h][2], BF16))
                if h == 0:
                    lhs.append(unpack_query(block, PARTS[h][2] * 7 // 2, BF16))
            term = jnp.dot(
                jnp.concatenate(lhs, axis=0),
                bout_v[pl.ds(j * 512, 512), :],
                preferred_element_type=F32,
            )
            total = term if total is None else total + term
        return total[: CHUNKS[h]], total[CHUNKS[h] :]

    def hop(h, way, step):
        index = h * 7 + way * 4 + step
        copy = pltpu.make_async_remote_copy(
            src_ref=(kept_a, kept_b)[way][h].at[step],
            dst_ref=(landed_a, landed_b)[way][h].at[step],
            send_sem=z_send.at[index],
            recv_sem=z_recv.at[index],
            device_id=((ahead, behind)[way], m),
            device_id_type=MESH,
        )
        copy.start()
        z_sent.append(copy)
        last[h, way] = copy

    products = {}
    turned = set()

    def product(h, step):
        products[h] = pair(h, ((4, -3), (3, -2), (2, -1), (1, 0))[step])

    def keep(h, ref, step, value):
        rows = PARTS[h][2]
        pack(ref, rows, value[:rows], (step,))
        if h == 0:
            query = value[rows:]
            high = query.astype(BF16).astype(F32)
            pack_query(ref, rows * 7 // 2, high, (step,))
            pack_query(ref, rows * 7 // 2 + 4 * RANK, query - high, (step,))

    def landed(h, ref, step):
        rows = PARTS[h][2]
        value = ref[step]
        tokens = unpack(value, rows, F32)
        if h:
            return tokens
        query = unpack_query(value, rows * 7 // 2, F32)
        query = query + unpack_query(value, rows * 7 // 2 + 4 * RANK, F32)
        return jnp.concatenate([tokens, query], axis=0)

    def reduce_step(h, step):
        if step == 0:
            gather_grads[h].rest()
            product(h, 0)
            a, b = products[h]
            keep(h, kept_a[h], 0, a)
            hop(h, 0, 0)
            keep(h, kept_b[h], 0, b)
            hop(h, 1, 0)
        elif step < 4:
            a, b = products[h]
            last[h, 0].wait_recv()
            keep(h, kept_a[h], step, a + landed(h, landed_a[h], step - 1))
            hop(h, 0, step)
            last[h, 1].wait_recv()
            b = b + landed(h, landed_b[h], step - 1)
            if step < 3:
                keep(h, kept_b[h], step, b)
                hop(h, 1, step)
            else:
                mine[h][...] = b
        else:
            last[h, 0].wait_recv()
            value = mine[h][...] + landed(h, landed_a[h], 3)
            s, first, rows = PARTS[h]
            pad[s, pl.ds(first, rows), :] = value[:rows]
            if s in turned:
                left[s] = pad[s].T.astype(BF16)
            turned.add(s)
            if h == 0:
                send_qout(value[rows:])

    my_rows = pl.ds(pl.multiple_of(z * RANK, RANK), RANK)
    qout_sent = []

    def send_qout(rotated_query):
        qout_all[my_rows, :] = rotated_query[:, :HID].astype(BF16)
        for o in range(1, PLANES):
            copy = pltpu.make_async_remote_copy(
                src_ref=qout_all.at[my_rows],
                dst_ref=qout_all.at[my_rows],
                send_sem=qout_send.at[o],
                recv_sem=qout_recv.at[o],
                device_id=(mod(z + o, PLANES), m),
                device_id_type=MESH,
            )
            copy.start()
            qout_sent.append(copy)

    arrived = set()

    def score(s, group):
        if group not in arrived:
            arrived.add(group)
            gather_wide.group(GROUPS[group])

        slots = group_slots(group)
        for k, slot in enumerate(slots):
            outer = jnp.dot(
                left[s, pl.ds(0, HID), :],
                wide_all[slot, pl.ds(s * LEN, 128), :],
                preferred_element_type=F32,
            )
            weighted[:, pl.ds(k * FEAT, FEAT)] = (outer * inverse[slot]).astype(BF16)
        queries = [wide_all[slot, pl.ds(TOKENS, QROWS), :] for slot in slots]
        mixed[s] += lax.dot_general(
            weighted[...],
            jnp.concatenate(queries, axis=1),
            (((1,), (1,)), ((), ())),
            preferred_element_type=F32,
        )

    def turn_queries():
        for copy in qout_sent:
            copy.wait_recv()
        pad[2, :, pl.ds(0, HID)] = qout_all[...].astype(F32)
        qout_t[...] = pad[2].T

    def start_wide():
        for copy in qin_sent:
            copy.wait_recv()
        run["W"]()

    scale = []

    def damp():
        scale.append(0.1 * jnp.sum(sum_last()) / (FF * D))

    run["W"], run["W0"] = run["W0"], start_wide
    for h, letter in enumerate(LETTERS):
        run["s" + letter] = functools.partial(one_of, shifts, shift[h].start, shift_here[h].start)
        run["r" + letter] = functools.partial(relay_block, h)
        run["t" + letter] = functools.partial(take_block, h)
        for step in range(5):
            run["z" + letter + str(step)] = functools.partial(reduce_step, h, step)
            run["p" + letter + str(step)] = functools.partial(product, h, step)
    for group in range(SIDE):
        run["rot" + str(group)] = functools.partial(rotate_group, group)
        run["inv" + str(group)] = functools.partial(invert, 8 * group, 8 * group + 8)
        for s in range(2):
            run["sc" + str(s) + str(group)] = functools.partial(score, s, group)
    run.update(eig=sum_eig, eig2=sum_second, turn=turn_basis, damp=damp, qt=turn_queries, rotd=rotated)

    mixed[...] = jnp.zeros_like(mixed)
    for name in SCHEDULE:
        run[name]()

    tiles2[0] = jnp.zeros((8, 128), F32)
    for s in range(2):
        tiles2[0, pl.ds(s, 1), :] = jnp.sum(
            mixed[s] * qout_t[pl.ds(0, HID), :], axis=0, keepdims=True
        )
    end_first, end_second, end_last, sum2_sent = plane_sum(
        place, tiles2, landed2, sum2_send, sum2_recv
    )
    end_first()
    end_second()
    out[...] = end_last()[:2]

    for gather in (gather_acts, *gather_grads, gather_wide):
        gather.finish()
    for copy in qin_sent + qout_sent + z_sent + sum1_sent + sum2_sent:
        copy.wait_send()


def per_device(
    activations, out_grads, valid_counts, basis_in, basis_out, eigvals, query_out, query_in
):
    anywhere = pl.BlockSpec(memory_space=pl.ANY)
    dma = pltpu.SemaphoreType.DMA
    vmem = pltpu.VMEM
    per_chunk = [[vmem((rows, HID), BF16) for rows in CHUNKS]]
    per_chunk += [[vmem((rows, 128), BF16) for rows in PACKED]] * 2
    per_chunk.append([vmem((DEVICES, rows, 128), BF16) for rows in PACKED])
    per_chunk += [[vmem((steps, rows, 128), BF16) for rows in SUMMED] for steps in (4, 3, 4, 3)]
    per_chunk.append([vmem((rows, 512), F32) for rows in CHUNKS])
    summed = pl.pallas_call(
        kernel,
        out_shape=jax.ShapeDtypeStruct((2, 128), F32),
        in_specs=[anywhere, anywhere, pl.BlockSpec(memory_space=pltpu.SMEM)] + [anywhere] * 5,
        out_specs=pl.BlockSpec(memory_space=pltpu.VMEM),
        scratch_shapes=[
            vmem((D, FEAT), BF16),
            vmem((512, 4 * HID), BF16),
            vmem((4 * 512, 512), BF16),
            vmem((HID, D), BF16),
            vmem((DEVICES, HID, FEAT), F32),
            vmem((DEVICES, ROWS, FEAT), BF16),
            vmem((DEVICES, WIDE, FEAT), BF16),
            vmem((ROWS, FEAT), F32),
            vmem((QROWS, HID), BF16),
            vmem((3, 128, 512), F32),
            vmem((2, 512, 128), BF16),
            vmem((512, 128), F32),
            vmem((2, HID, QROWS), F32),
            vmem((HID, 2 * SIDE * FEAT), BF16),
            vmem((2, 8, 128), F32),
            vmem((10, 8, 128), F32),
            vmem((2, 8, 128), F32),
            vmem((10, 8, 128), F32),
            *sum(per_chunk, []),
            dma((11,)),
            dma((6, len(CHUNKS))),
            *[dma((PLANES,))] * 4,
            *[dma((7 * len(CHUNKS),))] * 2,
            *[dma((10,))] * 4,
            *[dma((31,)), dma((32,))] * (2 + len(CHUNKS)),
        ],
        compiler_params=pltpu.CompilerParams(
            collective_id=0, has_side_effects=True, vmem_limit_bytes=60 * 1024 * 1024
        ),
    )(activations, out_grads, valid_counts, basis_in, basis_out.T, eigvals, query_out, query_in)
    return jnp.sum(summed.reshape(2, PLANES, RANK), axis=2)


def solution(mesh):
    in_specs = (
        P("grp", None, "mp"),
        P("grp", None, "mp"),
        P("grp"),
        P(None, "mp"),
        P("grp", "mp"),
        P("mp", None),
        P("grp", None, "mp"),
        P("grp", None, "mp"),
    )
    return jax.shard_map(
        per_device, mesh=mesh, in_specs=in_specs, out_specs=P("grp", None), check_vma=False
    )
```

```python
import functools

import jax
import jax.numpy as jnp
from jax import lax
from jax.experimental import pallas as pl
from jax.experimental.pallas import tpu as pltpu
from jax.sharding import PartitionSpec as P

MESH = pl.DeviceIdType.MESH
F32 = jnp.float32
BF16 = jnp.bfloat16

SIDE = 4
PLANES = 8
DEVICES = 32
TOKENS = 192
RANK = 16
ROWS = TOKENS + RANK
LEN = 96
HID = 448
FEAT = 256
QROWS = PLANES * RANK
WIDE = TOKENS + QROWS
FF = HID * DEVICES
D = FEAT * DEVICES


def mod(value, n):
    return lax.rem(value + 2 * n, n)


BOTH = (1, -1)
RING = (
    ((0, 0), BOTH, BOTH),
    ((-1, 0), (1,), BOTH),
    ((1, 0), (), BOTH),
    ((0, -1), (), (1,)),
    ((0, 1), (), ()),
    ((2, 0), (), BOTH),
    ((-1, -1), (), ()),
    ((-1, 1), (), (-1,)),
    ((1, -1), (), ()),
    ((1, 1), (), (-1,)),
    ((2, -1), (), (1,)),
    ((2, 1), (), ()),
    ((0, 2), (), ()),
    ((-1, 2), (), ()),
    ((1, 2), (), ()),
    ((2, 2), (), ()),
)
EARLY = (((0, 0), (1, -1, 2), BOTH), ((-1, 0), (), BOTH)) + RING[2:]
ALL = (1, -1, 2)
DIRECT = (((0, 0), ALL, ALL),) + tuple(((d1, 0), (), ALL) for d1 in (-1, 1, 2))
DIRECT += tuple(((d1, d2), (), ()) for d1 in (0, -1, 1, 2) for d2 in (-1, 1, 2))
GROUPS = (0, -1, 1, 2)


def slot_of(x, y, core, d1, d2):
    a = mod(x * (1 - core) + y * core + d1, SIDE)
    b = mod(y * (1 - core) + x * core + d2, SIDE)
    return ((a * (1 - core) + b * core) * SIDE + b * (1 - core) + a * core) * 2 + core


class Gather:
    def __init__(self, place, buf, send_sems, recv_sems):
        self.z, self.m, self.x, self.y, self.core = place
        self.buf, self.send_sems, self.recv_sems = buf, send_sems, recv_sems
        self.sibling = self.m + 1 - 2 * self.core
        self.sent = []

    def slot(self, d1, d2):
        return slot_of(self.x, self.y, self.core, d1, d2)

    def copy(self, slot, to, index):
        return pltpu.make_async_remote_copy(
            src_ref=self.buf.at[slot],
            dst_ref=self.buf.at[slot],
            send_sem=self.send_sems.at[index],
            recv_sem=self.recv_sems.at[slot],
            device_id=(self.z, to),
            device_id_type=MESH,
        )

    def send(self, slot, to):
        copy = self.copy(slot, to, len(self.sent))
        copy.start()
        self.sent.append(copy)

    def arrive(self, slot):
        self.copy(slot, self.sibling, 0).wait_recv()

    def event(self, offset, first=(), second=()):
        slot = self.slot(*offset)
        if offset != (0, 0):
            self.arrive(slot)
        for step in first:
            self.send(slot, self.slot(step, 0))
        for step in second:
            self.send(slot, self.slot(0, step))
        self.send(slot, self.sibling)

    def events(self, plan):
        return [functools.partial(self.event, *entry) for entry in plan]

    def group(self, d1):
        def body(d2, carry):
            self.arrive(slot_of(self.x, self.y, 1 - self.core, d1, d2))
            return carry

        lax.fori_loop(0, SIDE, body, 0)

    def rest(self):
        def body(chip, carry):
            self.arrive(chip * 2 + 1 - self.core)
            return carry

        lax.fori_loop(0, SIDE * SIDE, body, 0)

    def finish(self):
        for copy in self.sent:
            copy.wait_send()


def plane_sum(place, tiles, landed, send_sems, recv_sems):
    z = place[0]
    row, column = sum_peers(place)
    sent = []

    def exchange(stage, base, peers):
        for index, peer in enumerate(peers):
            copy = pltpu.make_async_remote_copy(
                src_ref=tiles.at[stage],
                dst_ref=landed.at[base + index],
                send_sem=send_sems.at[base + index],
                recv_sem=recv_sems.at[base + index],
                device_id=(z, peer),
                device_id_type=MESH,
            )
            copy.start()
            sent.append(copy)

    def collect(stage, base, peers):
        total = tiles[stage]
        for index in range(len(peers)):
            sent[base + index].wait_recv()
            total = total + landed[base + index]
        return total

    def first():
        exchange(0, 0, row)

    def second():
        tiles[1] = collect(0, 0, row)
        exchange(1, len(row), column)

    def last():
        return collect(1, len(row), column)

    return first, second, last, sent


def sum_peers(place):
    z, m, x, y, core = place
    row = []
    for ox in range(SIDE):
        for oc in range(2):
            if ox or oc:
                row.append((mod(x + ox, SIDE) * SIDE + y) * 2 + lax.rem(core + oc, 2))
    column = [(x * SIDE + mod(y + o, SIDE)) * 2 + core for o in (1, 2, 3)]
    return row, column


PLAN_A, PLAN_G, PLAN_W = EARLY, EARLY, RING
SCHEDULE = (
    "sG", "sH", "sI", "sJ", "A0", "eig", "rG", "rH", "rI", "rJ", "turn", "A1", "A2", "A5",
    "A3", "A4", "eig2", "tG", "G0", "A6", "A7", "A8", "A9", "tI", "I0", "A10", "A11", "G2",
    "A12", "damp", "inv0", "G1", "G4", "G5", "rot0", "G3", "A13", "tH", "H0", "I1", "inv1",
    "A14", "I2", "I3", "I5", "tJ", "J0", "A15", "I4", "rot1", "G8", "G9", "rot2", "G6", "G7",
    "rot3", "G10", "G11", "H2", "G12", "rotd", "H1", "H3", "H4", "H5", "I6", "I7", "I8", "I9",
    "I11", "I12", "J2", "I10", "J1", "G14", "J4", "J3", "J5", "G13", "H9", "G15", "H7", "H8",
    "H11", "H6", "inv2", "H10", "H12", "zG0", "pG1", "I13", "I14", "H14", "H13", "I15", "J6",
    "J7", "J8", "J9", "J10", "J11", "H15", "W0", "zI0", "pI1", "zH0", "pH1", "zG1", "pG2",
    "J12", "J13", "J14", "J15", "inv3", "W1", "W2", "zI1", "pI2", "zH1", "pH2", "zJ0", "pJ1",
    "W3", "W4", "zG2", "pG3", "W5", "zI2", "pI3", "zH2", "pH3", "zJ1", "pJ2", "W6", "W7", "W9",
    "zG3", "W8", "zI3", "W11", "W12", "zH3", "zJ2", "pJ3", "W13", "W10", "zG4", "zI4", "W14",
    "zH4", "sc00", "zJ3", "sc01", "qt", "W15", "sc02", "zJ4", "sc10", "sc03", "sc11", "sc12",
    "sc13",
)
PARTS = ((0, 0, 64), (0, 64, 32), (1, 0, 64), (1, 64, 32))
CHUNKS = tuple(rows + RANK * (h == 0) for h, (_, _, rows) in enumerate(PARTS))
PACKED = tuple(rows * 7 // 2 + 4 * RANK * (h == 0) for h, (_, _, rows) in enumerate(PARTS))
SUMMED = tuple(rows * 7 // 2 + 8 * RANK * (h == 0) for h, (_, _, rows) in enumerate(PARTS))
HALF_LANES = 64
LETTERS = "GHIJ"


def pack(ref, rows, value, at=()):
    value = value.astype(F32)
    for t in range(3):
        ref[(*at, pl.ds(t * rows, rows), slice(None))] = value[:, t * 128 : t * 128 + 128].astype(BF16)
    half = rows // 2
    first, second = value[:half, 384:], value[half:, 384:]
    lane = lax.broadcasted_iota(jnp.int32, (half, 128), 1)
    folded = jnp.where(lane < HALF_LANES, first, pltpu.roll(second, HALF_LANES, 1))
    ref[(*at, pl.ds(3 * rows, half), slice(None))] = folded.astype(BF16)


def unpack(value, rows, kind):
    tiles = [value[t * rows : t * rows + rows].astype(kind) for t in range(3)]
    folded = value[3 * rows : 3 * rows + rows // 2].astype(F32)
    last = jnp.concatenate([folded, pltpu.roll(folded, HALF_LANES, 1)], axis=0)
    return jnp.concatenate([*tiles, last.astype(kind)], axis=1)


def pack_query(ref, start, value, at=()):
    lane = lax.broadcasted_iota(jnp.int32, (RANK, 128), 1)
    for t in range(4):
        tile = value[:, t * 128 : t * 128 + 128].astype(F32)
        if t == 3:
            tile = jnp.where(lane < HALF_LANES, tile, 0.0)
        ref[(*at, pl.ds(start + t * RANK, RANK), slice(None))] = tile.astype(BF16)


def unpack_query(value, start, kind):
    tiles = [value[start + t * RANK : start + t * RANK + RANK] for t in range(4)]
    return jnp.concatenate(tiles, axis=1).astype(kind)


def kernel(
    acts,
    grads,
    counts,
    basis_in,
    basis_out,
    eigvals,
    query_out,
    query_in,
    out,
    *scratch,
):
    names = iter(scratch)
    bin_v, bout_t, bout_v, eig_v, inverse, acts_all, wide_all, acc_in = (next(names) for _ in range(8))
    qout_all, pad, left, qout_t, mixed, weighted = (next(names) for _ in range(6))
    tiles1, landed1, tiles2, landed2 = (next(names) for _ in range(4))
    raw, stage, relay, grads_all, kept_a, kept_b, landed_a, landed_b, mine = (
        [next(names) for _ in CHUNKS] for _ in range(9)
    )
    local_sems, perm_sems, qin_send, qin_recv, qout_send, qout_recv = (next(names) for _ in range(6))
    z_send, z_recv, sum1_send, sum1_recv, sum2_send, sum2_recv = (next(names) for _ in range(6))
    gather_sems = [(next(names), next(names)) for _ in range(6)]

    z = lax.axis_index("grp")
    m = lax.axis_index("mp")
    core = lax.rem(m, 2)
    chip = lax.div(m, 2)
    x, y = lax.div(chip, SIDE), lax.rem(chip, SIDE)
    place = (z, m, x, y, core)

    y_low, y_high = lax.rem(y, 2), lax.div(y, 2)

    def place_of(target, j_high, j_low, source):
        ring = mod(target - source - 4 * j_low, PLANES)
        high = lax.rem(ring, 2)
        low = lax.rem(j_high + lax.rem(target, 2) + high, 2)
        return (lax.div(ring, 2) * SIDE + 2 * high + low) * 2 + j_low

    x_relay = lax.div(mod(2 * x + y_high - z - 4 * core, PLANES), 2)
    relay_to = (x_relay * SIDE + y) * 2 + core
    ring = 2 * x + lax.rem(y_high + z, 2)
    plane = lax.rem(ring + z + 4 * core, PLANES)
    to = place_of(plane, y_low, core, z)
    from_plane = mod(z - (2 * x + y_high) - 4 * core, PLANES)
    from_y = 2 * lax.rem(z, 2) + lax.rem(y_low + y_high + lax.rem(z, 2), 2)
    from_device = (x * SIDE + from_y) * 2 + core
    shifts = x_relay != x
    stays = jnp.logical_and(plane == z, to == m)
    moves = jnp.logical_not(stays)

    barrier = pltpu.get_barrier_semaphore()
    row, column = sum_peers(place)
    for peer in row + column:
        pl.semaphore_signal(barrier, inc=1, device_id=(z, peer), device_id_type=MESH)
    for o in range(1, PLANES):
        pl.semaphore_signal(
            barrier, inc=1, device_id=(mod(z + o, PLANES), m), device_id_type=MESH
        )

    @pl.when(moves)
    def _():
        pl.semaphore_signal(
            barrier, inc=1, device_id=(from_plane, from_device), device_id_type=MESH
        )

    loads = []

    def load(src, dst):
        copy = pltpu.make_async_copy(src, dst, local_sems.at[len(loads)])
        copy.start()
        loads.append(copy)

    for h, (s, first, rows) in enumerate(PARTS):
        load(grads.at[s, pl.ds(first, rows)], raw[h].at[pl.ds(0, rows)])
    load(query_out.at[0], raw[0].at[pl.ds(PARTS[0][2], RANK)])
    load(acts.at[0], acts_all.at[m, pl.ds(0, LEN)])
    load(acts.at[1], acts_all.at[m, pl.ds(LEN, LEN)])
    load(query_in.at[0], acts_all.at[m, pl.ds(TOKENS, RANK)])
    first_loads = list(loads)
    load(eigvals, eig_v)
    load(basis_out, bout_t.at[pl.ds(0, HID)])
    load(basis_in, bin_v)
    load_eig, load_out, load_in = loads[-3:]

    pl.semaphore_wait(
        barrier, len(row) + len(column) + PLANES - 1 + jnp.where(stays, 0, 1)
    )

    shift, shift_here, permute, permute_here = [], [], [], []
    chunks = len(CHUNKS)
    for h in range(chunks):
        shift.append(
            pltpu.make_async_remote_copy(
                src_ref=stage[h],
                dst_ref=relay[h],
                send_sem=perm_sems.at[0, h],
                recv_sem=perm_sems.at[1, h],
                device_id=(z, relay_to),
                device_id_type=MESH,
            )
        )
        shift_here.append(pltpu.make_async_copy(stage[h], relay[h], perm_sems.at[2, h]))
        permute.append(
            pltpu.make_async_remote_copy(
                src_ref=relay[h],
                dst_ref=grads_all[h].at[to],
                send_sem=perm_sems.at[3, h],
                recv_sem=perm_sems.at[4, h],
                device_id=(plane, to),
                device_id_type=MESH,
            )
        )
        permute_here.append(
            pltpu.make_async_copy(relay[h], grads_all[h].at[m], perm_sems.at[5, h])
        )

    def one_of(predicate, yes, no):
        @pl.when(predicate)
        def _():
            yes()

        @pl.when(jnp.logical_not(predicate))
        def _():
            no()

    pad[...] = jnp.zeros_like(pad)

    def shift_block(h):
        first_loads[h].wait()
        if h == 0:
            first_loads[chunks].wait()
        pad[2, pl.ds(0, CHUNKS[h]), pl.ds(0, HID)] = raw[h][...].astype(F32)
        value = pad[2, pl.ds(0, CHUNKS[h]), :]
        rows = PARTS[h][2]
        pack(stage[h], rows, value[:rows])
        if h == 0:
            pack_query(stage[h], rows * 7 // 2, value[rows:])
        one_of(shifts, shift[h].start, shift_here[h].start)

    def start_acts():
        for copy in first_loads[chunks + 1 :]:
            copy.wait()
        run["A"]()

    gather_acts = Gather(place, acts_all, *gather_sems[0])
    gather_wide = Gather(place, wide_all, *gather_sems[1])
    gather_grads = [Gather(place, grads_all[h], *gather_sems[2 + h]) for h in range(chunks)]
    run = {}
    for letter, gather, plan in (
        ("A", gather_acts, PLAN_A),
        ("W", gather_wide, PLAN_W),
        *((letter, gather, PLAN_G) for letter, gather in zip(LETTERS, gather_grads)),
    ):
        for index, event in enumerate(gather.events(plan)):
            run[letter + str(index)] = event

    def relay_block(h):
        one_of(shifts, shift[h].wait, shift_here[h].wait)
        one_of(moves, permute[h].start, permute_here[h].start)

    def take_block(h):
        one_of(moves, permute[h].wait, permute_here[h].wait)

    sum_first, sum_second, sum_last, sum1_sent = plane_sum(
        place, tiles1, landed1, sum1_send, sum1_recv
    )

    def sum_eig():
        load_eig.wait()

        def add_eig(slot, total):
            columns = pl.ds(pl.multiple_of(slot * FEAT, FEAT), FEAT)
            block = eig_v[:, columns].astype(F32).reshape(HID // 8, 8, FEAT)
            return total + jnp.sum(block, axis=0)

        eig_sum = lax.fori_loop(0, DEVICES, add_eig, jnp.zeros((8, FEAT), F32))
        tiles1[0] = eig_sum[:, :128] + eig_sum[:, 128:]
        sum_first()

    def turn_basis():
        load_out.wait()

        bout_t[pl.ds(HID, 512 - HID), :] = jnp.zeros((512 - HID, 4 * HID), BF16)

        def turn(i, carry):
            turned = bout_t[:, pl.ds(pl.multiple_of(i * 128, 128), 128)].astype(F32).T.astype(BF16)
            for k in range(2):
                piece = 2 * i + k
                row = lax.div(piece, 7) * 512 + lax.rem(piece, 7) * HALF_LANES
                rows = pl.ds(pl.multiple_of(row, HALF_LANES), HALF_LANES)
                bout_v[rows, :] = turned[k * HALF_LANES : (k + 1) * HALF_LANES]
            return carry

        lax.fori_loop(0, 4 * HID // 128, turn, 0)
        for j in range(4):
            rows = pl.ds(j * 512 + HID, 512 - HID)
            bout_v[rows, :] = jnp.zeros((512 - HID, 512), BF16)

    def invert(start, stop):
        def body(slot, carry):
            columns = pl.ds(pl.multiple_of(slot * FEAT, FEAT), FEAT)
            inverse[slot] = 1.0 / (eig_v[:, columns].astype(F32) + scale[0])
            return carry

        lax.fori_loop(start, stop, body, 0)

    qin_sent = []
    my_query = pl.ds(pl.multiple_of(TOKENS + z * RANK, RANK), RANK)

    def group_slots(group):
        return [
            slot_of(x, y, lax.rem(core + k, 2), GROUPS[group], k // 2) for k in range(2 * SIDE)
        ]

    def rotate_group(group):
        gather_acts.group(GROUPS[group])
        if group == 0:
            load_in.wait()
            acc_in[...] = jnp.zeros_like(acc_in)

        total = None
        for slot in group_slots(group):
            rows = pl.ds(pl.multiple_of(slot * FEAT, FEAT), FEAT)
            term = jnp.dot(acts_all[slot], bin_v[rows, :], preferred_element_type=F32)
            total = term if total is None else total + term
        acc_in[...] += total

    def rotated():
        position = lax.broadcasted_iota(jnp.int32, (LEN, FEAT), 0)
        for s in range(2):
            rows = pl.ds(s * LEN, LEN)
            kept = jnp.where(position < counts[s], acc_in[rows, :], 0.0)
            wide_all[m, rows, :] = kept.astype(BF16)
        wide_all[m, my_query, :] = acc_in[pl.ds(TOKENS, RANK), :].astype(BF16)
        for o in range(1, PLANES):
            copy = pltpu.make_async_remote_copy(
                src_ref=wide_all.at[m, my_query],
                dst_ref=wide_all.at[m, my_query],
                send_sem=qin_send.at[o],
                recv_sem=qin_recv.at[o],
                device_id=(mod(z + o, PLANES), m),
                device_id_type=MESH,
            )
            copy.start()
            qin_sent.append(copy)

    toward = 1 - 2 * core
    ahead = mod(z + toward, PLANES)
    behind = mod(z - toward, PLANES)
    z_sent = []
    last = {}

    def pair(h, offsets):
        total = None
        slots = [mod(z + toward * offset, PLANES) for offset in offsets]
        for j in range(4):
            lhs = []
            for source in slots:
                block = grads_all[h][place_of(z, j // 2, j % 2, source)]
                lhs.append(unpack(block, PARTS[h][2], BF16))
                if h == 0:
                    lhs.append(unpack_query(block, PARTS[h][2] * 7 // 2, BF16))
            term = jnp.dot(
                jnp.concatenate(lhs, axis=0),
                bout_v[pl.ds(j * 512, 512), :],
                preferred_element_type=F32,
            )
            total = term if total is None else total + term
        return total[: CHUNKS[h]], total[CHUNKS[h] :]

    def hop(h, way, step):
        index = h * 7 + way * 4 + step
        copy = pltpu.make_async_remote_copy(
            src_ref=(kept_a, kept_b)[way][h].at[step],
            dst_ref=(landed_a, landed_b)[way][h].at[step],
            send_sem=z_send.at[index],
            recv_sem=z_recv.at[index],
            device_id=((ahead, behind)[way], m),
            device_id_type=MESH,
        )
        copy.start()
        z_sent.append(copy)
        last[h, way] = copy

    products = {}
    turned = set()

    def product(h, step):
        products[h] = pair(h, ((4, -3), (3, -2), (2, -1), (1, 0))[step])

    def keep(h, ref, step, value):
        rows = PARTS[h][2]
        pack(ref, rows, value[:rows], (step,))
        if h == 0:
            query = value[rows:]
            high = query.astype(BF16).astype(F32)
            pack_query(ref, rows * 7 // 2, high, (step,))
            pack_query(ref, rows * 7 // 2 + 4 * RANK, query - high, (step,))

    def landed(h, ref, step):
        rows = PARTS[h][2]
        value = ref[step]
        tokens = unpack(value, rows, F32)
        if h:
            return tokens
        query = unpack_query(value, rows * 7 // 2, F32)
        query = query + unpack_query(value, rows * 7 // 2 + 4 * RANK, F32)
        return jnp.concatenate([tokens, query], axis=0)

    def reduce_step(h, step):
        if step == 0:
            gather_grads[h].rest()
            product(h, 0)
            a, b = products[h]
            keep(h, kept_a[h], 0, a)
            hop(h, 0, 0)
            keep(h, kept_b[h], 0, b)
            hop(h, 1, 0)
        elif step < 4:
            a, b = products[h]
            last[h, 0].wait_recv()
            keep(h, kept_a[h], step, a + landed(h, landed_a[h], step - 1))
            hop(h, 0, step)
            last[h, 1].wait_recv()
            b = b + landed(h, landed_b[h], step - 1)
            if step < 3:
                keep(h, kept_b[h], step, b)
                hop(h, 1, step)
            else:
                mine[h][...] = b
        else:
            last[h, 0].wait_recv()
            value = mine[h][...] + landed(h, landed_a[h], 3)
            s, first, rows = PARTS[h]
            pad[s, pl.ds(first, rows), :] = value[:rows]
            if s in turned:
                left[s] = pad[s].T.astype(BF16)
            turned.add(s)
            if h == 0:
                send_qout(value[rows:])

    my_rows = pl.ds(pl.multiple_of(z * RANK, RANK), RANK)
    qout_sent = []

    def send_qout(rotated_query):
        qout_all[my_rows, :] = rotated_query[:, :HID].astype(BF16)
        for o in range(1, PLANES):
            copy = pltpu.make_async_remote_copy(
                src_ref=qout_all.at[my_rows],
                dst_ref=qout_all.at[my_rows],
                send_sem=qout_send.at[o],
                recv_sem=qout_recv.at[o],
                device_id=(mod(z + o, PLANES), m),
                device_id_type=MESH,
            )
            copy.start()
            qout_sent.append(copy)

    arrived = set()

    def score(s, group):
        if group not in arrived:
            arrived.add(group)
            gather_wide.group(GROUPS[group])

        slots = group_slots(group)
        for k, slot in enumerate(slots):
            outer = jnp.dot(
                left[s, pl.ds(0, HID), :],
                wide_all[slot, pl.ds(s * LEN, 128), :],
                preferred_element_type=F32,
            )
            weighted[:, pl.ds(k * FEAT, FEAT)] = (outer * inverse[slot]).astype(BF16)
        queries = [wide_all[slot, pl.ds(TOKENS, QROWS), :] for slot in slots]
        mixed[s] += lax.dot_general(
            weighted[...],
            jnp.concatenate(queries, axis=1),
            (((1,), (1,)), ((), ())),
            preferred_element_type=F32,
        )

    def turn_queries():
        for copy in qout_sent:
            copy.wait_recv()
        pad[2, :, pl.ds(0, HID)] = qout_all[...].astype(F32)
        qout_t[...] = pad[2].T

    def start_wide():
        for copy in qin_sent:
            copy.wait_recv()
        run["W"]()

    scale = []

    def damp():
        scale.append(0.1 * jnp.sum(sum_last()) / (FF * D))

    run["W"], run["W0"] = run["W0"], start_wide
    run["A"], run["A0"] = run["A0"], start_acts
    for h, letter in enumerate(LETTERS):
        run["s" + letter] = functools.partial(shift_block, h)
        run["r" + letter] = functools.partial(relay_block, h)
        run["t" + letter] = functools.partial(take_block, h)
        for step in range(5):
            run["z" + letter + str(step)] = functools.partial(reduce_step, h, step)
            run["p" + letter + str(step)] = functools.partial(product, h, step)
    for group in range(SIDE):
        run["rot" + str(group)] = functools.partial(rotate_group, group)
        run["inv" + str(group)] = functools.partial(invert, 8 * group, 8 * group + 8)
        for s in range(2):
            run["sc" + str(s) + str(group)] = functools.partial(score, s, group)
    run.update(eig=sum_eig, eig2=sum_second, turn=turn_basis, damp=damp, qt=turn_queries, rotd=rotated)

    mixed[...] = jnp.zeros_like(mixed)
    for name in SCHEDULE:
        run[name]()

    tiles2[0] = jnp.zeros((8, 128), F32)
    for s in range(2):
        tiles2[0, pl.ds(s, 1), :] = jnp.sum(
            mixed[s] * qout_t[pl.ds(0, HID), :], axis=0, keepdims=True
        )
    end_first, end_second, end_last, sum2_sent = plane_sum(
        place, tiles2, landed2, sum2_send, sum2_recv
    )
    end_first()
    end_second()
    out[...] = end_last()[:2]

    for gather in (gather_acts, *gather_grads, gather_wide):
        gather.finish()
    for copy in qin_sent + qout_sent + z_sent + sum1_sent + sum2_sent:
        copy.wait_send()


def per_device(
    activations, out_grads, valid_counts, basis_in, basis_out, eigvals, query_out, query_in
):
    anywhere = pl.BlockSpec(memory_space=pl.ANY)
    dma = pltpu.SemaphoreType.DMA
    vmem = pltpu.VMEM
    per_chunk = [[vmem((rows, HID), BF16) for rows in CHUNKS]]
    per_chunk += [[vmem((rows, 128), BF16) for rows in PACKED]] * 2
    per_chunk.append([vmem((DEVICES, rows, 128), BF16) for rows in PACKED])
    per_chunk += [[vmem((steps, rows, 128), BF16) for rows in SUMMED] for steps in (4, 3, 4, 3)]
    per_chunk.append([vmem((rows, 512), F32) for rows in CHUNKS])
    summed = pl.pallas_call(
        kernel,
        out_shape=jax.ShapeDtypeStruct((2, 128), F32),
        in_specs=[anywhere, anywhere, pl.BlockSpec(memory_space=pltpu.SMEM)] + [anywhere] * 5,
        out_specs=pl.BlockSpec(memory_space=pltpu.VMEM),
        scratch_shapes=[
            vmem((D, FEAT), BF16),
            vmem((512, 4 * HID), BF16),
            vmem((4 * 512, 512), BF16),
            vmem((HID, D), BF16),
            vmem((DEVICES, HID, FEAT), F32),
            vmem((DEVICES, ROWS, FEAT), BF16),
            vmem((DEVICES, WIDE, FEAT), BF16),
            vmem((ROWS, FEAT), F32),
            vmem((QROWS, HID), BF16),
            vmem((3, 128, 512), F32),
            vmem((2, 512, 128), BF16),
            vmem((512, 128), F32),
            vmem((2, HID, QROWS), F32),
            vmem((HID, 2 * SIDE * FEAT), BF16),
            vmem((2, 8, 128), F32),
            vmem((10, 8, 128), F32),
            vmem((2, 8, 128), F32),
            vmem((10, 8, 128), F32),
            *sum(per_chunk, []),
            dma((11,)),
            dma((6, len(CHUNKS))),
            *[dma((PLANES,))] * 4,
            *[dma((7 * len(CHUNKS),))] * 2,
            *[dma((10,))] * 4,
            *[dma((31,)), dma((32,))] * (2 + len(CHUNKS)),
        ],
        compiler_params=pltpu.CompilerParams(
            collective_id=0, has_side_effects=True, vmem_limit_bytes=60 * 1024 * 1024
        ),
    )(activations, out_grads, valid_counts, basis_in, basis_out.T, eigvals, query_out, query_in)
    return jnp.sum(summed.reshape(2, PLANES, RANK), axis=2)


def solution(mesh):
    in_specs = (
        P("grp", None, "mp"),
        P("grp", None, "mp"),
        P("grp"),
        P(None, "mp"),
        P("grp", "mp"),
        P("mp", None),
        P("grp", None, "mp"),
        P("grp", None, "mp"),
    )
    return jax.shard_map(
        per_device, mesh=mesh, in_specs=in_specs, out_specs=P("grp", None), check_vma=False
    )
```

```python
import functools

import jax
import jax.numpy as jnp
from jax import lax
from jax.experimental import pallas as pl
from jax.experimental.pallas import tpu as pltpu
from jax.sharding import PartitionSpec as P

MESH = pl.DeviceIdType.MESH
F32 = jnp.float32
BF16 = jnp.bfloat16

SIDE = 4
PLANES = 8
DEVICES = 32
TOKENS = 192
RANK = 16
ROWS = TOKENS + RANK
LEN = 96
HID = 448
FEAT = 256
QROWS = PLANES * RANK
WIDE = TOKENS + QROWS
FF = HID * DEVICES
D = FEAT * DEVICES


def mod(value, n):
    return lax.rem(value + 2 * n, n)


BOTH = (1, -1)
RING = (
    ((0, 0), BOTH, BOTH),
    ((-1, 0), (1,), BOTH),
    ((1, 0), (), BOTH),
    ((0, -1), (), (1,)),
    ((0, 1), (), ()),
    ((2, 0), (), BOTH),
    ((-1, -1), (), ()),
    ((-1, 1), (), (-1,)),
    ((1, -1), (), ()),
    ((1, 1), (), (-1,)),
    ((2, -1), (), (1,)),
    ((2, 1), (), ()),
    ((0, 2), (), ()),
    ((-1, 2), (), ()),
    ((1, 2), (), ()),
    ((2, 2), (), ()),
)
EARLY = (((0, 0), (1, -1, 2), BOTH), ((-1, 0), (), BOTH)) + RING[2:]
ALL = (1, -1, 2)
DIRECT = (((0, 0), ALL, ALL),) + tuple(((d1, 0), (), ALL) for d1 in (-1, 1, 2))
DIRECT += tuple(((d1, d2), (), ()) for d1 in (0, -1, 1, 2) for d2 in (-1, 1, 2))
GROUPS = (0, -1, 1, 2)


def slot_of(x, y, core, d1, d2):
    a = mod(x * (1 - core) + y * core + d1, SIDE)
    b = mod(y * (1 - core) + x * core + d2, SIDE)
    return ((a * (1 - core) + b * core) * SIDE + b * (1 - core) + a * core) * 2 + core


class Gather:
    def __init__(self, place, buf, send_sems, recv_sems):
        self.z, self.m, self.x, self.y, self.core = place
        self.buf, self.send_sems, self.recv_sems = buf, send_sems, recv_sems
        self.sibling = self.m + 1 - 2 * self.core
        self.sent = []

    def slot(self, d1, d2):
        return slot_of(self.x, self.y, self.core, d1, d2)

    def copy(self, slot, to, index):
        return pltpu.make_async_remote_copy(
            src_ref=self.buf.at[slot],
            dst_ref=self.buf.at[slot],
            send_sem=self.send_sems.at[index],
            recv_sem=self.recv_sems.at[slot],
            device_id=(self.z, to),
            device_id_type=MESH,
        )

    def send(self, slot, to):
        copy = self.copy(slot, to, len(self.sent))
        copy.start()
        self.sent.append(copy)

    def arrive(self, slot):
        self.copy(slot, self.sibling, 0).wait_recv()

    def event(self, offset, first=(), second=()):
        slot = self.slot(*offset)
        if offset != (0, 0):
            self.arrive(slot)
        for step in first:
            self.send(slot, self.slot(step, 0))
        for step in second:
            self.send(slot, self.slot(0, step))
        self.send(slot, self.sibling)

    def events(self, plan):
        return [functools.partial(self.event, *entry) for entry in plan]

    def group(self, d1):
        def body(d2, carry):
            self.arrive(slot_of(self.x, self.y, 1 - self.core, d1, d2))
            return carry

        lax.fori_loop(0, SIDE, body, 0)

    def rest(self):
        def body(chip, carry):
            self.arrive(chip * 2 + 1 - self.core)
            return carry

        lax.fori_loop(0, SIDE * SIDE, body, 0)

    def finish(self):
        for copy in self.sent:
            copy.wait_send()


def plane_sum(place, tiles, landed, send_sems, recv_sems):
    z = place[0]
    row, column = sum_peers(place)
    sent = []

    def exchange(stage, base, peers):
        for index, peer in enumerate(peers):
            copy = pltpu.make_async_remote_copy(
                src_ref=tiles.at[stage],
                dst_ref=landed.at[base + index],
                send_sem=send_sems.at[base + index],
                recv_sem=recv_sems.at[base + index],
                device_id=(z, peer),
                device_id_type=MESH,
            )
            copy.start()
            sent.append(copy)

    def collect(stage, base, peers):
        total = tiles[stage]
        for index in range(len(peers)):
            sent[base + index].wait_recv()
            total = total + landed[base + index]
        return total

    def first():
        exchange(0, 0, row)

    def second():
        tiles[1] = collect(0, 0, row)
        exchange(1, len(row), column)

    def last():
        return collect(1, len(row), column)

    return first, second, last, sent


def sum_peers(place):
    z, m, x, y, core = place
    row = []
    for ox in range(SIDE):
        for oc in range(2):
            if ox or oc:
                row.append((mod(x + ox, SIDE) * SIDE + y) * 2 + lax.rem(core + oc, 2))
    column = [(x * SIDE + mod(y + o, SIDE)) * 2 + core for o in (1, 2, 3)]
    return row, column


PLAN_A, PLAN_G, PLAN_W = EARLY, EARLY, RING
SCHEDULE = (
    "sG", "sH", "sI", "sJ", "A0", "eig", "rG", "rH", "rI", "rJ", "turn", "A1", "A2", "A5",
    "A3", "A4", "eig2", "tG", "G0", "A6", "A7", "A8", "A9", "tI", "I0", "A10", "A11", "G2",
    "A12", "damp", "inv0", "G1", "G4", "G5", "rot0", "G3", "A13", "tH", "H0", "I1", "inv1",
    "A14", "I2", "I3", "I5", "tJ", "J0", "A15", "I4", "rot1", "G8", "G9", "rot2", "G6", "G7",
    "rot3", "G10", "G11", "H2", "G12", "rotd", "H1", "H3", "H4", "H5", "I6", "I7", "I8", "I9",
    "I11", "I12", "J2", "I10", "J1", "G14", "J4", "J3", "J5", "G13", "H9", "G15", "H7", "H8",
    "H11", "H6", "inv2", "H10", "H12", "zG0", "pG1", "I13", "I14", "H14", "H13", "I15", "J6",
    "J7", "J8", "J9", "J10", "J11", "H15", "W0", "zI0", "pI1", "zH0", "pH1", "zG1", "pG2",
    "J12", "J13", "J14", "J15", "inv3", "W1", "W2", "zI1", "pI2", "zH1", "pH2", "zJ0", "pJ1",
    "W3", "W4", "zG2", "pG3", "W5", "zI2", "pI3", "zH2", "pH3", "zJ1", "pJ2", "W6", "W7", "W9",
    "zG3", "W8", "zI3", "W11", "W12", "zH3", "zJ2", "pJ3", "W13", "W10", "zG4", "zI4", "W14",
    "zH4", "sc00", "zJ3", "sc01", "qt", "W15", "sc02", "zJ4", "sc10", "sc03", "sc11", "sc12",
    "sc13",
)
PARTS = ((0, 0, 64), (0, 64, 32), (1, 0, 64), (1, 64, 32))
CHUNKS = tuple(rows + RANK * (h == 0) for h, (_, _, rows) in enumerate(PARTS))
PACKED = tuple(rows * 7 // 2 + 4 * RANK * (h == 0) for h, (_, _, rows) in enumerate(PARTS))
SUMMED = tuple(rows * 7 // 2 + 8 * RANK * (h == 0) for h, (_, _, rows) in enumerate(PARTS))
HALF_LANES = 64
LETTERS = "GHIJ"


def pack(ref, rows, value, at=()):
    value = value.astype(F32)
    for t in range(3):
        ref[(*at, pl.ds(t * rows, rows), slice(None))] = value[:, t * 128 : t * 128 + 128].astype(BF16)
    half = rows // 2
    first, second = value[:half, 384:], value[half:, 384:]
    lane = lax.broadcasted_iota(jnp.int32, (half, 128), 1)
    folded = jnp.where(lane < HALF_LANES, first, pltpu.roll(second, HALF_LANES, 1))
    ref[(*at, pl.ds(3 * rows, half), slice(None))] = folded.astype(BF16)


def unpack(value, rows, kind):
    tiles = [value[t * rows : t * rows + rows].astype(kind) for t in range(3)]
    folded = value[3 * rows : 3 * rows + rows // 2].astype(F32)
    last = jnp.concatenate([folded, pltpu.roll(folded, HALF_LANES, 1)], axis=0)
    return jnp.concatenate([*tiles, last.astype(kind)], axis=1)


def pack_query(ref, start, value, at=()):
    lane = lax.broadcasted_iota(jnp.int32, (RANK, 128), 1)
    for t in range(4):
        tile = value[:, t * 128 : t * 128 + 128].astype(F32)
        if t == 3:
            tile = jnp.where(lane < HALF_LANES, tile, 0.0)
        ref[(*at, pl.ds(start + t * RANK, RANK), slice(None))] = tile.astype(BF16)


def unpack_query(value, start, kind):
    tiles = [value[start + t * RANK : start + t * RANK + RANK] for t in range(4)]
    return jnp.concatenate(tiles, axis=1).astype(kind)


def kernel(
    acts,
    grads,
    counts,
    basis_in,
    basis_out,
    eigvals,
    query_out,
    query_in,
    out,
    *scratch,
):
    names = iter(scratch)
    bin_v, bout_t, bout_v, eig_v, inverse, acts_all, wide_all, acc_in = (next(names) for _ in range(8))
    qout_all, pad, left, qout_t, mixed, weighted = (next(names) for _ in range(6))
    tiles1, landed1, tiles2, landed2 = (next(names) for _ in range(4))
    raw, stage, relay, grads_all, kept_a, kept_b, landed_a, landed_b, mine = (
        [next(names) for _ in CHUNKS] for _ in range(9)
    )
    local_sems, perm_sems, qin_send, qin_recv, qout_send, qout_recv = (next(names) for _ in range(6))
    z_send, z_recv, sum1_send, sum1_recv, sum2_send, sum2_recv = (next(names) for _ in range(6))
    gather_sems = [(next(names), next(names)) for _ in range(6)]

    z = lax.axis_index("grp")
    m = lax.axis_index("mp")
    core = lax.rem(m, 2)
    chip = lax.div(m, 2)
    x, y = lax.div(chip, SIDE), lax.rem(chip, SIDE)
    place = (z, m, x, y, core)

    y_low, y_high = lax.rem(y, 2), lax.div(y, 2)

    def place_of(target, j_high, j_low, source):
        ring = mod(target - source - 4 * j_low, PLANES)
        high = lax.rem(ring, 2)
        low = lax.rem(j_high + lax.rem(target, 2) + high, 2)
        return (lax.div(ring, 2) * SIDE + 2 * high + low) * 2 + j_low

    x_relay = lax.div(mod(2 * x + y_high - z - 4 * core, PLANES), 2)
    relay_to = (x_relay * SIDE + y) * 2 + core
    ring = 2 * x + lax.rem(y_high + z, 2)
    plane = lax.rem(ring + z + 4 * core, PLANES)
    to = place_of(plane, y_low, core, z)
    from_plane = mod(z - (2 * x + y_high) - 4 * core, PLANES)
    from_y = 2 * lax.rem(z, 2) + lax.rem(y_low + y_high + lax.rem(z, 2), 2)
    from_device = (x * SIDE + from_y) * 2 + core
    shifts = x_relay != x
    stays = jnp.logical_and(plane == z, to == m)
    moves = jnp.logical_not(stays)

    barrier = pltpu.get_barrier_semaphore()
    row, column = sum_peers(place)
    for peer in row + column:
        pl.semaphore_signal(barrier, inc=1, device_id=(z, peer), device_id_type=MESH)
    for o in range(1, PLANES):
        pl.semaphore_signal(
            barrier, inc=1, device_id=(mod(z + o, PLANES), m), device_id_type=MESH
        )

    @pl.when(moves)
    def _():
        pl.semaphore_signal(
            barrier, inc=1, device_id=(from_plane, from_device), device_id_type=MESH
        )

    loads = []

    def load(src, dst):
        copy = pltpu.make_async_copy(src, dst, local_sems.at[len(loads)])
        copy.start()
        loads.append(copy)

    for h, (s, first, rows) in enumerate(PARTS):
        load(grads.at[s, pl.ds(first, rows)], raw[h].at[pl.ds(0, rows)])
    load(query_out.at[0], raw[0].at[pl.ds(PARTS[0][2], RANK)])
    load(acts.at[0], acts_all.at[m, pl.ds(0, LEN)])
    load(acts.at[1], acts_all.at[m, pl.ds(LEN, LEN)])
    load(query_in.at[0], acts_all.at[m, pl.ds(TOKENS, RANK)])
    first_loads = list(loads)
    load(eigvals, eig_v)
    load(basis_out, bout_t.at[pl.ds(0, HID)])
    load(basis_in, bin_v)
    load_eig, load_out, load_in = loads[-3:]

    pl.semaphore_wait(
        barrier, len(row) + len(column) + PLANES - 1 + jnp.where(stays, 0, 1)
    )

    shift, shift_here, permute, permute_here = [], [], [], []
    chunks = len(CHUNKS)
    for h in range(chunks):
        shift.append(
            pltpu.make_async_remote_copy(
                src_ref=stage[h],
                dst_ref=relay[h],
                send_sem=perm_sems.at[0, h],
                recv_sem=perm_sems.at[1, h],
                device_id=(z, relay_to),
                device_id_type=MESH,
            )
        )
        shift_here.append(pltpu.make_async_copy(stage[h], relay[h], perm_sems.at[2, h]))
        permute.append(
            pltpu.make_async_remote_copy(
                src_ref=relay[h],
                dst_ref=grads_all[h].at[to],
                send_sem=perm_sems.at[3, h],
                recv_sem=perm_sems.at[4, h],
                device_id=(plane, to),
                device_id_type=MESH,
            )
        )
        permute_here.append(
            pltpu.make_async_copy(relay[h], grads_all[h].at[m], perm_sems.at[5, h])
        )

    def one_of(predicate, yes, no):
        @pl.when(predicate)
        def _():
            yes()

        @pl.when(jnp.logical_not(predicate))
        def _():
            no()

    pad[...] = jnp.zeros_like(pad)

    def shift_block(h):
        first_loads[h].wait()
        if h == 0:
            first_loads[chunks].wait()
        pad[2, pl.ds(0, CHUNKS[h]), pl.ds(0, HID)] = raw[h][...].astype(F32)
        value = pad[2, pl.ds(0, CHUNKS[h]), :]
        rows = PARTS[h][2]
        pack(stage[h], rows, value[:rows])
        if h == 0:
            pack_query(stage[h], rows * 7 // 2, value[rows:])
        one_of(shifts, shift[h].start, shift_here[h].start)

    def start_acts():
        for copy in first_loads[chunks + 1 :]:
            copy.wait()
        run["A"]()

    gather_acts = Gather(place, acts_all, *gather_sems[0])
    gather_wide = Gather(place, wide_all, *gather_sems[1])
    gather_grads = [Gather(place, grads_all[h], *gather_sems[2 + h]) for h in range(chunks)]
    run = {}
    for letter, gather, plan in (
        ("A", gather_acts, PLAN_A),
        ("W", gather_wide, PLAN_W),
        *((letter, gather, PLAN_G) for letter, gather in zip(LETTERS, gather_grads)),
    ):
        for index, event in enumerate(gather.events(plan)):
            run[letter + str(index)] = event

    def relay_block(h):
        one_of(shifts, shift[h].wait, shift_here[h].wait)
        one_of(moves, permute[h].start, permute_here[h].start)

    def take_block(h):
        one_of(moves, permute[h].wait, permute_here[h].wait)

    sum_first, sum_second, sum_last, sum1_sent = plane_sum(
        place, tiles1, landed1, sum1_send, sum1_recv
    )

    def sum_eig():
        load_eig.wait()

        def add_eig(slot, total):
            columns = pl.ds(pl.multiple_of(slot * FEAT, FEAT), FEAT)
            block = eig_v[:, columns].astype(F32).reshape(HID // 8, 8, FEAT)
            return total + jnp.sum(block, axis=0)

        eig_sum = lax.fori_loop(0, DEVICES, add_eig, jnp.zeros((8, FEAT), F32))
        tiles1[0] = eig_sum[:, :128] + eig_sum[:, 128:]
        sum_first()

    def turn_basis():
        load_out.wait()

        bout_t[pl.ds(HID, 512 - HID), :] = jnp.zeros((512 - HID, 4 * HID), BF16)

        def turn(i, carry):
            turned = bout_t[:, pl.ds(pl.multiple_of(i * 128, 128), 128)].astype(F32).T.astype(BF16)
            for k in range(2):
                piece = 2 * i + k
                row = lax.div(piece, 7) * 512 + lax.rem(piece, 7) * HALF_LANES
                rows = pl.ds(pl.multiple_of(row, HALF_LANES), HALF_LANES)
                bout_v[rows, :] = turned[k * HALF_LANES : (k + 1) * HALF_LANES]
            return carry

        lax.fori_loop(0, 4 * HID // 128, turn, 0)
        for j in range(4):
            rows = pl.ds(j * 512 + HID, 512 - HID)
            bout_v[rows, :] = jnp.zeros((512 - HID, 512), BF16)

    def invert(start, stop):
        def body(slot, carry):
            columns = pl.ds(pl.multiple_of(slot * FEAT, FEAT), FEAT)
            inverse[slot] = 1.0 / (eig_v[:, columns].astype(F32) + scale[0])
            return carry

        lax.fori_loop(start, stop, body, 0)

    qin_sent = []
    my_query = pl.ds(pl.multiple_of(TOKENS + z * RANK, RANK), RANK)

    def group_slots(group):
        return [
            slot_of(x, y, lax.rem(core + k, 2), GROUPS[group], k // 2) for k in range(2 * SIDE)
        ]

    def rotate_group(group):
        gather_acts.group(GROUPS[group])
        if group == 0:
            load_in.wait()
            acc_in[...] = jnp.zeros_like(acc_in)

        total = None
        for slot in group_slots(group):
            rows = pl.ds(pl.multiple_of(slot * FEAT, FEAT), FEAT)
            term = jnp.dot(acts_all[slot], bin_v[rows, :], preferred_element_type=F32)
            total = term if total is None else total + term
        acc_in[...] += total

    def rotated():
        position = lax.broadcasted_iota(jnp.int32, (LEN, FEAT), 0)
        for s in range(2):
            rows = pl.ds(s * LEN, LEN)
            kept = jnp.where(position < counts[s], acc_in[rows, :], 0.0)
            wide_all[m, rows, :] = kept.astype(BF16)
        wide_all[m, my_query, :] = acc_in[pl.ds(TOKENS, RANK), :].astype(BF16)
        for o in range(1, PLANES):
            copy = pltpu.make_async_remote_copy(
                src_ref=wide_all.at[m, my_query],
                dst_ref=wide_all.at[m, my_query],
                send_sem=qin_send.at[o],
                recv_sem=qin_recv.at[o],
                device_id=(mod(z + o, PLANES), m),
                device_id_type=MESH,
            )
            copy.start()
            qin_sent.append(copy)

    toward = 1 - 2 * core
    ahead = mod(z + toward, PLANES)
    behind = mod(z - toward, PLANES)
    z_sent = []
    last = {}

    def pair(h, offsets):
        total = None
        slots = [mod(z + toward * offset, PLANES) for offset in offsets]
        for j in range(4):
            lhs = []
            for source in slots:
                block = grads_all[h][place_of(z, j // 2, j % 2, source)]
                lhs.append(unpack(block, PARTS[h][2], BF16))
                if h == 0:
                    lhs.append(unpack_query(block, PARTS[h][2] * 7 // 2, BF16))
            term = jnp.dot(
                jnp.concatenate(lhs, axis=0),
                bout_v[pl.ds(j * 512, 512), :],
                preferred_element_type=F32,
            )
            total = term if total is None else total + term
        return total[: CHUNKS[h]], total[CHUNKS[h] :]

    def hop(h, way, step):
        index = h * 7 + way * 4 + step
        copy = pltpu.make_async_remote_copy(
            src_ref=(kept_a, kept_b)[way][h].at[step],
            dst_ref=(landed_a, landed_b)[way][h].at[step],
            send_sem=z_send.at[index],
            recv_sem=z_recv.at[index],
            device_id=((ahead, behind)[way], m),
            device_id_type=MESH,
        )
        copy.start()
        z_sent.append(copy)
        last[h, way] = copy

    products = {}
    turned = set()

    def product(h, step):
        products[h] = pair(h, ((4, -3), (3, -2), (2, -1), (1, 0))[step])

    def keep(h, ref, step, value):
        rows = PARTS[h][2]
        pack(ref, rows, value[:rows], (step,))
        if h == 0:
            query = value[rows:]
            high = query.astype(BF16).astype(F32)
            pack_query(ref, rows * 7 // 2, high, (step,))
            pack_query(ref, rows * 7 // 2 + 4 * RANK, query - high, (step,))

    def landed(h, ref, step):
        rows = PARTS[h][2]
        value = ref[step]
        tokens = unpack(value, rows, F32)
        if h:
            return tokens
        query = unpack_query(value, rows * 7 // 2, F32)
        query = query + unpack_query(value, rows * 7 // 2 + 4 * RANK, F32)
        return jnp.concatenate([tokens, query], axis=0)

    def reduce_step(h, step):
        if step == 0:
            gather_grads[h].rest()
            product(h, 0)
            a, b = products[h]
            keep(h, kept_a[h], 0, a)
            hop(h, 0, 0)
            keep(h, kept_b[h], 0, b)
            hop(h, 1, 0)
        elif step < 4:
            a, b = products[h]
            last[h, 0].wait_recv()
            keep(h, kept_a[h], step, a + landed(h, landed_a[h], step - 1))
            hop(h, 0, step)
            last[h, 1].wait_recv()
            b = b + landed(h, landed_b[h], step - 1)
            if step < 3:
                keep(h, kept_b[h], step, b)
                hop(h, 1, step)
            else:
                mine[h][...] = b
        else:
            last[h, 0].wait_recv()
            value = mine[h][...] + landed(h, landed_a[h], 3)
            s, first, rows = PARTS[h]
            pad[s, pl.ds(first, rows), :] = value[:rows]
            if s in turned:
                left[s] = pad[s].T.astype(BF16)
            turned.add(s)
            if h == 0:
                send_qout(value[rows:])

    my_rows = pl.ds(pl.multiple_of(z * RANK, RANK), RANK)
    qout_sent = []

    def send_qout(rotated_query):
        qout_all[my_rows, :] = rotated_query[:, :HID].astype(BF16)
        for o in range(1, PLANES):
            copy = pltpu.make_async_remote_copy(
                src_ref=qout_all.at[my_rows],
                dst_ref=qout_all.at[my_rows],
                send_sem=qout_send.at[o],
                recv_sem=qout_recv.at[o],
                device_id=(mod(z + o, PLANES), m),
                device_id_type=MESH,
            )
            copy.start()
            qout_sent.append(copy)

    arrived = set()

    def score(s, group):
        if group not in arrived:
            arrived.add(group)
            gather_wide.group(GROUPS[group])

        slots = group_slots(group)
        for k, slot in enumerate(slots):
            outer = jnp.dot(
                left[s, pl.ds(0, HID), :],
                wide_all[slot, pl.ds(s * LEN, 128), :],
                preferred_element_type=F32,
            )
            weighted[:, pl.ds(k * FEAT, FEAT)] = (outer * inverse[slot]).astype(BF16)
        queries = [wide_all[slot, pl.ds(TOKENS, QROWS), :] for slot in slots]
        mixed[s] += lax.dot_general(
            weighted[...],
            jnp.concatenate(queries, axis=1),
            (((1,), (1,)), ((), ())),
            preferred_element_type=F32,
        )

    def turn_queries():
        for copy in qout_sent:
            copy.wait_recv()
        pad[2, :, pl.ds(0, HID)] = qout_all[...].astype(F32)
        qout_t[...] = pad[2].T

    def start_wide():
        for copy in qin_sent:
            copy.wait_recv()
        run["W"]()

    scale = []

    def damp():
        scale.append(0.1 * jnp.sum(sum_last()) / (FF * D))

    run["W"], run["W0"] = run["W0"], start_wide
    run["A"], run["A0"] = run["A0"], start_acts
    for h, letter in enumerate(LETTERS):
        run["s" + letter] = functools.partial(shift_block, h)
        run["r" + letter] = functools.partial(relay_block, h)
        run["t" + letter] = functools.partial(take_block, h)
        for step in range(5):
            run["z" + letter + str(step)] = functools.partial(reduce_step, h, step)
            run["p" + letter + str(step)] = functools.partial(product, h, step)
    for group in range(SIDE):
        run["rot" + str(group)] = functools.partial(rotate_group, group)
        run["inv" + str(group)] = functools.partial(invert, 8 * group, 8 * group + 8)
        for s in range(2):
            run["sc" + str(s) + str(group)] = functools.partial(score, s, group)
    run.update(eig=sum_eig, eig2=sum_second, turn=turn_basis, damp=damp, qt=turn_queries, rotd=rotated)

    mixed[...] = jnp.zeros_like(mixed)
    for name in SCHEDULE:
        run[name]()

    tiles2[0] = jnp.zeros((8, 128), F32)
    for s in range(2):
        tiles2[0, pl.ds(s, 1), :] = jnp.sum(
            mixed[s] * qout_t[pl.ds(0, HID), :], axis=0, keepdims=True
        )
    end_first, end_second, end_last, sum2_sent = plane_sum(
        place, tiles2, landed2, sum2_send, sum2_recv
    )
    end_first()
    for gather in (gather_acts, *gather_grads[:2]):
        gather.finish()
    for copy in qin_sent + qout_sent + sum1_sent:
        copy.wait_send()
    end_second()
    for gather in (*gather_grads[2:], gather_wide):
        gather.finish()
    for copy in z_sent:
        copy.wait_send()
    out[...] = end_last()[:2]
    for copy in sum2_sent:
        copy.wait_send()


def per_device(
    activations, out_grads, valid_counts, basis_in, basis_out, eigvals, query_out, query_in
):
    anywhere = pl.BlockSpec(memory_space=pl.ANY)
    dma = pltpu.SemaphoreType.DMA
    vmem = pltpu.VMEM
    per_chunk = [[vmem((rows, HID), BF16) for rows in CHUNKS]]
    per_chunk += [[vmem((rows, 128), BF16) for rows in PACKED]] * 2
    per_chunk.append([vmem((DEVICES, rows, 128), BF16) for rows in PACKED])
    per_chunk += [[vmem((steps, rows, 128), BF16) for rows in SUMMED] for steps in (4, 3, 4, 3)]
    per_chunk.append([vmem((rows, 512), F32) for rows in CHUNKS])
    summed = pl.pallas_call(
        kernel,
        out_shape=jax.ShapeDtypeStruct((2, 128), F32),
        in_specs=[anywhere, anywhere, pl.BlockSpec(memory_space=pltpu.SMEM)] + [anywhere] * 5,
        out_specs=pl.BlockSpec(memory_space=pltpu.VMEM),
        scratch_shapes=[
            vmem((D, FEAT), BF16),
            vmem((512, 4 * HID), BF16),
            vmem((4 * 512, 512), BF16),
            vmem((HID, D), BF16),
            vmem((DEVICES, HID, FEAT), F32),
            vmem((DEVICES, ROWS, FEAT), BF16),
            vmem((DEVICES, WIDE, FEAT), BF16),
            vmem((ROWS, FEAT), F32),
            vmem((QROWS, HID), BF16),
            vmem((3, 128, 512), F32),
            vmem((2, 512, 128), BF16),
            vmem((512, 128), F32),
            vmem((2, HID, QROWS), F32),
            vmem((HID, 2 * SIDE * FEAT), BF16),
            vmem((2, 8, 128), F32),
            vmem((10, 8, 128), F32),
            vmem((2, 8, 128), F32),
            vmem((10, 8, 128), F32),
            *sum(per_chunk, []),
            dma((11,)),
            dma((6, len(CHUNKS))),
            *[dma((PLANES,))] * 4,
            *[dma((7 * len(CHUNKS),))] * 2,
            *[dma((10,))] * 4,
            *[dma((31,)), dma((32,))] * (2 + len(CHUNKS)),
        ],
        compiler_params=pltpu.CompilerParams(
            collective_id=0, has_side_effects=True, vmem_limit_bytes=60 * 1024 * 1024
        ),
    )(activations, out_grads, valid_counts, basis_in, basis_out.T, eigvals, query_out, query_in)
    return jnp.sum(summed.reshape(2, PLANES, RANK), axis=2)


def solution(mesh):
    in_specs = (
        P("grp", None, "mp"),
        P("grp", None, "mp"),
        P("grp"),
        P(None, "mp"),
        P("grp", "mp"),
        P("mp", None),
        P("grp", None, "mp"),
        P("grp", None, "mp"),
    )
    return jax.shard_map(
        per_device, mesh=mesh, in_specs=in_specs, out_specs=P("grp", None), check_vma=False
    )
```
